128 devices in a mesh: blk: 32 (over y_hi, x, z), uly: 4 (over y_lo, core).
Axes of the slice: x: 4, y: 4 (y_hi: 2, y_lo: 2; y = y_hi * 2 + y_lo), z: 4, core: 2. Of those that a mesh axis runs over, the one named last changes fastest.
Arguments:
- cond_query: bfloat16 [6144, 2560], P('blk', 'uly'), may hold values from -100 to 100
- cond_kv: bfloat16 [2, 6144, 2560], P(None, 'blk', 'uly'), may hold values from -100 to 100
- uncond_qkv: bfloat16 [3, 6144, 2560], P(None, ('blk', 'uly')), may hold values from -100 to 100
- uncond_cache: bfloat16 [6144, 2560], P(('blk', 'uly')), may hold values from -2 to 2
- refresh: int32 [6144], P(('blk', 'uly')), may hold values 0 or 1
- valid: int32 [32], replicated, may hold values from 48 to 192, as said below
Outputs:
- guided: bfloat16 [6144, 2560], P(('blk', 'uly'))
- new_cache: bfloat16 [6144, 2560], P(('blk', 'uly'))
The draws below stay inside these ranges and needn't reach their ends.
Inputs may be any that keep to these rules, and one draw needn't show every extreme that they name: `valid`: every shard holds at least a quarter of its slots; some shard is full in every draw.
All inputs are finite; a program needn't handle non-finite values. No bound on the sum of `refresh` on one device may be relied on, other than what follows from the above.
Results may differ from the reference program's by a relative error of at most 0.012.
Values may be sent and summed in bfloat16 or wider, within the bound.
A program may use at most 192 MiB of HBM per device.

```python
import math
import jax
import jax.numpy as jnp
from jax import lax

H = 20
HD = 128
TOK_BLK = 192
SHARDS = 32
TOKENS = 6144


def row_scale(key, lower_bound, upper_bound):
    return jnp.exp(jax.random.uniform(key, (TOKENS, 1), jnp.float32, math.log(lower_bound), math.log(upper_bound)))


def attention_inputs(key):
    columns = H * HD
    pieces = jax.random.split(key, 6)
    query = jax.random.normal(pieces[0], (TOKENS, columns), jnp.float32)
    raw_keys = jax.random.normal(pieces[1], (TOKENS, columns), jnp.float32)
    values = jax.random.normal(pieces[2], (TOKENS, columns), jnp.float32)
    query = query * row_scale(pieces[3], 0.15, 1.5)
    keys = raw_keys * row_scale(pieces[4], 0.3, 3.0)
    values = values * row_scale(pieces[5], 1.0, 10.0)
    return (query, keys, values)


def draw_cond_query(key, part):
    triple = attention_inputs(key)
    return triple[0].astype(jnp.bfloat16)


def draw_cond_kv(key, part):
    triple = attention_inputs(key)
    return jnp.stack([triple[1], triple[2]]).astype(jnp.bfloat16)


def draw_uncond_qkv(key, part):
    triple = attention_inputs(jax.random.fold_in(key, 7))
    return jnp.stack([triple[0], triple[1], triple[2]]).astype(jnp.bfloat16)


def draw_valid(key, part):
    key = jax.random.fold_in(key, 11)
    counts = jax.random.randint(key, (SHARDS,), TOK_BLK // 4, TOK_BLK + 1, jnp.int32)
    filled = jax.random.randint(jax.random.fold_in(key, 1), (), 0, SHARDS, jnp.int32)
    return jnp.where(jnp.arange(SHARDS, dtype=jnp.int32) == filled, TOK_BLK, counts).astype(jnp.int32)


def set_ends(values, own_key, low, high):
    longest = values.shape.index(max(values.shape))
    spots = []
    for shift in (0, 1):
        where = [jax.random.randint(jax.random.fold_in(own_key, axis), (), 0, length) for axis, length in enumerate(values.shape)]
        where[longest] = (where[longest] + shift) % values.shape[longest]
        spots.append(tuple(where))
    return values.at[spots[0]].set(low).at[spots[1]].set(high)


def shard_levels(rng, shape, cuts, least, high):
    factor_of, own = 1.0, jax.random.fold_in(rng, 6)
    for dim, parts in cuts:
        heights = jnp.exp(jax.random.uniform(jax.random.fold_in(own, dim), (parts,), jnp.float32, least / len(cuts), high / len(cuts)))
        factor_of = factor_of * jnp.repeat(heights, shape[dim] // parts).reshape([-1 if axis == dim else 1 for axis in range(len(shape))])
    return factor_of


def gaussian(key, extent, width, bound, cuts=(), held_as=jnp.bfloat16):
    drawn = jax.random.normal(key, extent, jnp.float32) * width
    if len(cuts) > 0:
        drawn = shard_levels(key, extent, cuts, -0.22, 0.18) * drawn
    return jnp.clip(drawn, min=-bound, max=bound).astype(held_as)


def setup_inputs(seed: int = 0) -> dict:
    splits = jax.random.split(jax.random.key(seed), 7)
    return {
        "cond_query": draw_cond_query(jax.random.fold_in(splits[6], 71), 0),
        "cond_kv": draw_cond_kv(jax.random.fold_in(splits[6], 71), 0),
        "uncond_qkv": draw_uncond_qkv(jax.random.fold_in(splits[6], 71), 0),
        "uncond_cache": gaussian(splits[3], (TOKENS, H * HD), 0.3, 2.0, ((0, 128),)),
        "refresh": set_ends((jax.random.randint(splits[4], (TOKENS,), 0, 2) < 1).astype(jnp.int32), jax.random.fold_in(splits[4], 1), 0, 1),
        "valid": draw_valid(jax.random.fold_in(splits[6], 71), 0),
    }


guidance = 5.0


def attention(query, keys, values, usable):
    query_heads = jnp.transpose(query.reshape(TOKENS, H, HD), (1, 0, 2))
    key_heads = jnp.transpose(keys.reshape(TOKENS, H, HD), (1, 0, 2))
    value_heads = jnp.transpose(values.reshape(TOKENS, H, HD), (1, 0, 2))

    def one_head(triple):
        head_query, head_keys, head_values = triple
        scores = jnp.dot(head_query, jnp.transpose(head_keys), preferred_element_type=jnp.float32) * (HD ** -0.5)
        scores = jnp.where(usable[None, :], scores, -1e30)
        row_max = jnp.max(scores, axis=1, keepdims=True)
        weights = jnp.where(usable[None, :], jnp.exp(scores - row_max), 0.0)
        denominator = jnp.sum(weights, axis=1, keepdims=True)
        summed = jnp.dot(weights.astype(jnp.bfloat16), head_values, preferred_element_type=jnp.float32)
        return summed / denominator

    outputs = lax.map(one_head, (query_heads, key_heads, value_heads))
    return jnp.transpose(outputs, (1, 0, 2)).reshape(TOKENS, H * HD).astype(jnp.bfloat16)


def reference(cond_query, cond_kv, uncond_qkv, uncond_cache, refresh, valid):
    places = jnp.arange(TOKENS, dtype=jnp.int32)
    owners = places // TOK_BLK
    usable = (places % TOK_BLK) < valid[owners]
    conditional = attention(cond_query, cond_kv[0], cond_kv[1], usable)
    fresh = attention(uncond_qkv[0], uncond_qkv[1], uncond_qkv[2], usable)
    new_cache = jnp.where(refresh[:, None] == 1, fresh, uncond_cache)
    chosen = new_cache.astype(jnp.float32)
    guided = (chosen + guidance * (conditional.astype(jnp.float32) - chosen)).astype(jnp.bfloat16)
    return guided, new_cache
```

```python
import functools

import jax
import jax.numpy as jnp
from jax import lax
from jax.experimental import pallas as pl
from jax.experimental.pallas import tpu as pltpu
from jax.sharding import PartitionSpec as P

HD = 128
GUIDANCE = 5.0
MESH = pl.DeviceIdType.MESH
LOG2E = 1.4426950408889634
SCALE = LOG2E * HD ** (-0.5)
UNUSABLE = -1e30

HEADS = 5
SHARD = 192
PIECE = 48
PAIR = 2 * SHARD
ALL = 4 * PAIR
TILE = 256
CHUNK = 256
NT = (((1,), (1,)), ((), ()))


def place():
    blk, uly = lax.axis_index("blk"), lax.axis_index("uly")
    return blk // 16, (blk // 4) % 4, blk % 4, uly


def kernel(
    valid_ref, q_hbm, kv_hbm, qkv_hbm, out_ref,
    q_all, kv_all, vt, bias, ones, scores, o_send, o_recv, st_send, st_recv, stage,
    y_ssem, y_rsem, y_lsem, x_ssem, x_rsem, z_ssem, z_rsem, o_ssem, o_rsem, f_ssem, f_rsem, f_lsem,
):
    hi, x, z, uly = place()
    me = hi * 4 + uly
    my_x = pl.multiple_of(x * PAIR, PAIR)
    my_z = pl.multiple_of(z * PAIR, PAIR)

    def column(member):
        return ((member // 4) * 16 + x * 4 + z, member % 4)

    def along_x(step):
        return (hi * 16 + lax.rem(x + step, 4) * 4 + z, uly)

    def along_z(step):
        return (hi * 16 + x * 4 + lax.rem(z + step, 4), uly)

    barrier = pltpu.get_barrier_semaphore()
    for step in range(1, 8):
        pl.semaphore_signal(barrier, inc=1, device_id=column(lax.rem(me + step, 8)), device_id_type=MESH)
    for step in range(1, 4):
        pl.semaphore_signal(barrier, inc=1, device_id=along_x(step), device_id_type=MESH)
        pl.semaphore_signal(barrier, inc=1, device_id=along_z(step), device_id_type=MESH)

    def head_columns(head):
        return pl.ds(head * HD, HD)

    def cond_own(head):
        return (
            pltpu.make_async_copy(
                q_hbm.at[:, head_columns(head)], q_all.at[head, pl.ds(my_z, SHARD)], y_lsem.at[head, 0]),
            pltpu.make_async_copy(
                kv_hbm.at[:, :, head_columns(head)], kv_all.at[head, :, pl.ds(my_x, SHARD)], y_lsem.at[head, 1]),
        )

    def cond_far(head):
        to = column(uly)
        return (
            pltpu.make_async_remote_copy(
                q_hbm.at[:, head_columns(head)], q_all.at[head, pl.ds(my_z + SHARD, SHARD)],
                y_ssem.at[head, 4, 0], y_rsem.at[head, 8, 0], device_id=to, device_id_type=MESH),
            pltpu.make_async_remote_copy(
                kv_hbm.at[:, :, head_columns(head)], kv_all.at[head, :, pl.ds(my_x + SHARD, SHARD)],
                y_ssem.at[head, 4, 1], y_rsem.at[head, 8, 1], device_id=to, device_id_type=MESH),
        )

    def uncond_refs(head, group, source):
        columns = pl.ds(pl.multiple_of((group * HEADS + head) * HD, HD), HD)
        row = pl.multiple_of(source * PIECE, PIECE)
        return (
            (qkv_hbm.at[0, :, columns], q_all.at[head, pl.ds(my_z + row, PIECE)]),
            (qkv_hbm.at[pl.ds(1, 2), :, columns], kv_all.at[head, :, pl.ds(my_x + row, PIECE)]),
        )

    def uncond_own(head):
        return tuple(
            pltpu.make_async_copy(src, dst, y_lsem.at[head, i])
            for i, (src, dst) in enumerate(uncond_refs(head, uly, me)))

    def uncond_far(head, group, source):
        return tuple(
            pltpu.make_async_remote_copy(
                src, dst, y_ssem.at[head, group, i], y_rsem.at[head, source, i],
                device_id=column(4 + group), device_id_type=MESH)
            for i, (src, dst) in enumerate(uncond_refs(head, group, source)))

    def y_start(head):
        @pl.when(hi == 0)
        def _():
            for copy in cond_own(head):
                copy.start()

        @pl.when(hi == 1)
        def _():
            for copy in cond_far(head):
                copy.start()
            for copy in uncond_own(head):
                copy.start()

        for group in range(4):
            @pl.when(me != 4 + group)
            def _():
                for copy in uncond_far(head, group, me):
                    copy.start()

    def y_wait(head):
        @pl.when(hi == 0)
        def _():
            for copy in cond_own(head):
                copy.wait()
            for copy in cond_far(head):
                copy.wait_recv()

        @pl.when(hi == 1)
        def _():
            for copy in uncond_own(head):
                copy.wait()
            for source in range(8):
                @pl.when(me != source)
                def _():
                    for copy in uncond_far(head, 0, source):
                        copy.wait_recv()

    def y_sent(head):
        @pl.when(hi == 1)
        def _():
            for copy in cond_far(head):
                copy.wait_send()

        for group in range(4):
            @pl.when(me != 4 + group)
            def _():
                for copy in uncond_far(head, group, me):
                    copy.wait_send()

    def gathers(head, from_x, from_z):
        copies = []
        for step in (2, 1, 3):
            block = kv_all.at[head, :, pl.ds(from_x(step), PAIR)]
            copies.append(pltpu.make_async_remote_copy(
                block, block, x_ssem.at[head, step - 1], x_rsem.at[head, step - 1],
                device_id=along_x(step), device_id_type=MESH))
            block = q_all.at[head, pl.ds(from_z(step), PAIR)]
            copies.append(pltpu.make_async_remote_copy(
                block, block, z_ssem.at[head, step - 1], z_rsem.at[head, step - 1],
                device_id=along_z(step), device_id_type=MESH))
        return copies

    def gathers_out(head):
        return gathers(head, lambda step: my_x, lambda step: my_z)

    def gathers_in(head):
        return gathers(
            head,
            lambda step: pl.multiple_of(lax.rem(x + 4 - step, 4) * PAIR, PAIR),
            lambda step: pl.multiple_of(lax.rem(z + 4 - step, 4) * PAIR, PAIR))

    def o_copies(head, step):
        lanes = pl.ds(pl.multiple_of(lax.rem(z + step, 4) * PAIR, PAIR), PAIR)
        return (
            pltpu.make_async_remote_copy(
                o_send.at[head, :, lanes], o_recv.at[head, step - 1], o_ssem.at[head, step - 1, 0],
                o_rsem.at[head, step - 1, 0], device_id=along_z(step), device_id_type=MESH),
            pltpu.make_async_remote_copy(
                st_send.at[head, :, lanes], st_recv.at[head, step - 1], o_ssem.at[head, step - 1, 1],
                o_rsem.at[head, step - 1, 1], device_id=along_z(step), device_id_type=MESH),
        )

    def final_refs(head, target, branch, group):
        columns = pl.ds(pl.multiple_of((group * HEADS + head) * HD, HD), HD)
        row = pl.multiple_of(target * PIECE, PIECE)
        return stage.at[head, pl.ds(row, PIECE)], out_ref.at[branch, :, columns]

    def final_own(head):
        src, dst = final_refs(head, me, hi, uly)
        return pltpu.make_async_copy(src, dst, f_lsem.at[head])

    def final_far(head, step):
        target = lax.rem(me + step, 8)
        src, dst = final_refs(head, target, hi, uly)
        return pltpu.make_async_remote_copy(
            src, dst, f_ssem.at[head, step - 1], f_rsem.at[head, step - 1],
            device_id=column(target), device_id_type=MESH)

    def prepare():
        lane = lax.broadcasted_iota(jnp.int32, (SHARD, HD), 1)
        row = lax.broadcasted_iota(jnp.int32, (SHARD, HD), 0)
        for slot in range(4):
            for half in range(2):
                present = valid_ref[half * 16 + slot * 4 + z]
                block = jnp.where((row >= present) & (lane == 0), UNUSABLE, 0.0)
                bias[pl.ds(slot * PAIR + half * SHARD, SHARD), :] = block.astype(jnp.bfloat16)
        ones[...] = jnp.where(
            lax.broadcasted_iota(jnp.int32, (TILE, HD), 1) == 0, 1.0, 0.0).astype(jnp.bfloat16)
        vt[pl.ds(HD, 16), :] = jnp.ones((16, ALL), jnp.bfloat16)

    def transpose_values(head):
        rows = lax.broadcasted_iota(jnp.int32, (HD, HD), 0)
        lanes = lax.broadcasted_iota(jnp.int32, (HD, HD), 1)
        eye = (rows == lanes).astype(jnp.bfloat16)
        for chunk in range(ALL // CHUNK):
            span = pl.ds(chunk * CHUNK, CHUNK)
            vt[pl.ds(0, HD), span] = lax.dot_general(
                eye, kv_all[head, 1, span, :], NT, preferred_element_type=jnp.float32).astype(jnp.bfloat16)

    def tile(head, start):
        start = pl.multiple_of(start, TILE)
        queries = jnp.concatenate([q_all[head, pl.ds(start, TILE), :], ones[...]], axis=1)
        top = None
        for chunk in range(ALL // CHUNK):
            span = pl.ds(chunk * CHUNK, CHUNK)
            keys = jnp.concatenate([kv_all[head, 0, span, :], bias[span, :]], axis=1)
            part = lax.dot_general(keys, queries, NT, preferred_element_type=jnp.float32)
            scores[span, :] = part
            part_top = jnp.max(part, axis=0, keepdims=True)
            top = part_top if top is None else jnp.maximum(top, part_top)
        total = jnp.zeros((HD + 16, TILE), jnp.float32)
        for chunk in range(ALL // CHUNK):
            span = pl.ds(chunk * CHUNK, CHUNK)
            weights = jnp.exp2((scores[span, :] - top) * SCALE).astype(jnp.bfloat16)
            total = total + jnp.dot(vt[:, span], weights, preferred_element_type=jnp.float32)
        o_send[head, :, pl.ds(start, TILE)] = total[:HD].astype(jnp.bfloat16)
        st_send[head, pl.ds(0, 1), pl.ds(start, TILE)] = top
        st_send[head, pl.ds(1, 1), pl.ds(start, TILE)] = total[HD:HD + 1]

    def compute(head):
        transpose_values(head)
        mine = z // 2
        for part in range(2):
            half = 1 - mine if part == 0 else mine

            def body(i, _):
                tile(head, half * (2 * PAIR) + i * TILE)
                return 0

            lax.fori_loop(0, 2 * PAIR // TILE, body, 0)
            for step in range(1, 4):
                target = lax.rem(z + step, 4)

                @pl.when(target // 2 == half)
                def _():
                    for copy in o_copies(head, step):
                        copy.start()

    def merge(head):
        for step in range(1, 4):
            for copy in o_copies(head, step):
                copy.wait_recv()
        own = pl.ds(my_z, PAIR)
        tops = [st_send[head, pl.ds(0, 1), own]] + [st_recv[head, i, pl.ds(0, 1), :] for i in range(3)]
        sums = [st_send[head, pl.ds(1, 1), own]] + [st_recv[head, i, pl.ds(1, 1), :] for i in range(3)]
        parts = [o_send[head, :, own]] + [o_recv[head, i] for i in range(3)]
        top = functools.reduce(jnp.maximum, tops)
        factors = [jnp.exp2((t - top) * SCALE) for t in tops]
        denominator = sum(f * s for f, s in zip(factors, sums))
        numerator = sum(f * p.astype(jnp.float32) for f, p in zip(factors, parts))
        stage[head] = (numerator / denominator).T.astype(jnp.bfloat16)
        final_own(head).start()
        for step in range(1, 8):
            final_far(head, step).start()

    def spread(head):
        y_wait(head)
        for copy in gathers_out(head):
            copy.start()
        if head + 2 < HEADS:
            y_start(head + 2)

    prepare()
    pl.semaphore_wait(barrier, 13)
    y_start(0)
    y_start(1)
    spread(0)
    spread(1)
    for head in range(HEADS):
        for copy in gathers_in(head):
            copy.wait_recv()
        compute(head)
        if head + 2 < HEADS:
            spread(head + 2)
        if head >= 1:
            merge(head - 1)
    merge(HEADS - 1)

    for head in range(HEADS):
        y_sent(head)
        for copy in gathers_out(head):
            copy.wait_send()
        for step in range(1, 4):
            for copy in o_copies(head, step):
                copy.wait_send()
        final_own(head).wait()
        for step in range(1, 8):
            final_far(head, step).wait()


def attend(cond_query, cond_kv, uncond_qkv, valid):
    any_space = pl.BlockSpec(memory_space=pl.ANY)
    dma = pltpu.SemaphoreType.DMA
    return pl.pallas_call(
        kernel,
        out_shape=jax.ShapeDtypeStruct((2, PIECE, 4 * HEADS * HD), jnp.bfloat16),
        in_specs=[pl.BlockSpec(memory_space=pltpu.SMEM), any_space, any_space, any_space],
        out_specs=any_space,
        scratch_shapes=[
            pltpu.VMEM((HEADS, ALL, HD), jnp.bfloat16),
            pltpu.VMEM((HEADS, 2, ALL, HD), jnp.bfloat16),
            pltpu.VMEM((HD + 16, ALL), jnp.bfloat16),
            pltpu.VMEM((ALL, HD), jnp.bfloat16),
            pltpu.VMEM((TILE, HD), jnp.bfloat16),
            pltpu.VMEM((ALL, TILE), jnp.float32),
            pltpu.VMEM((HEADS, HD, ALL), jnp.bfloat16),
            pltpu.VMEM((HEADS, 3, HD, PAIR), jnp.bfloat16),
            pltpu.VMEM((HEADS, 8, ALL), jnp.float32),
            pltpu.VMEM((HEADS, 3, 8, PAIR), jnp.float32),
            pltpu.VMEM((HEADS, PAIR, HD), jnp.bfloat16),
            dma((HEADS, 5, 2)), dma((HEADS, 9, 2)), dma((HEADS, 2)),
            dma((HEADS, 3)), dma((HEADS, 3)),
            dma((HEADS, 3)), dma((HEADS, 3)),
            dma((HEADS, 3, 2)), dma((HEADS, 3, 2)),
            dma((HEADS, 7)), dma((HEADS, 7)), dma((HEADS,)),
        ],
        compiler_params=pltpu.CompilerParams(
            collective_id=0, has_side_effects=True, vmem_limit_bytes=40 << 20),
    )(valid, cond_query, cond_kv, uncond_qkv)


def on_device(cond_query, cond_kv, uncond_qkv, uncond_cache, refresh, valid):
    tokens = attend(cond_query, cond_kv, uncond_qkv, valid)
    new_cache = jnp.where(refresh[:, None] == 1, tokens[1], uncond_cache)
    chosen = new_cache.astype(jnp.float32)
    guided = (chosen + GUIDANCE * (tokens[0].astype(jnp.float32) - chosen)).astype(jnp.bfloat16)
    return (guided, new_cache)


def solution(mesh):
    placed = (
        P("blk", "uly"),
        P(None, "blk", "uly"),
        P(None, ("blk", "uly"), None),
        P(("blk", "uly"), None),
        P(("blk", "uly")),
        P(),
    )
    return jax.shard_map(
        on_device,
        mesh=mesh,
        in_specs=placed,
        out_specs=(P(("blk", "uly"), None), P(("blk", "uly"), None)),
        check_vma=False,
    )
```

```python
import functools

import jax
import jax.numpy as jnp
from jax import lax
from jax.experimental import pallas as pl
from jax.experimental.pallas import tpu as pltpu
from jax.sharding import PartitionSpec as P

HD = 128
GUIDANCE = 5.0
MESH = pl.DeviceIdType.MESH
LOG2E = 1.4426950408889634
SCALE = LOG2E * HD ** (-0.5)
UNUSABLE = -1e30

HALF = HD // 2
HEADS = 5
LAST = HEADS - 1
WIDTH = HEADS * HD
UNITS = ((0, 1), (1, 1), (2, 1), (3, 2))
SHARD = 192
PIECE = 48
PAIR = 2 * SHARD
ALL = 4 * PAIR
TILE = 256
NT = (((1,), (1,)), ((), ()))
STEPS = (0, 3, 2, 1)


def slot_rows(slot):
    return pl.ds(slot * PAIR, PAIR)


def head_lanes(head):
    return pl.ds(pl.multiple_of(head * HD, HD), HD)


def kernel(
    valid_ref, q_hbm, kv_hbm, qkv_hbm, cache_ref, refresh_ref, guided_out, cache_out,
    qkv, vt, bias, ones, scores_even, scores_odd, partial, tops, stats,
    o_send, st_send, o_half_in, st_half_in, o_full, o_full_in, st_full, st_full_in, o_recv, st_recv, stage, tokens,
    y_sem, g_sem, o_sem, d_sem, f_sem, y_sent, g_sent, o_sent, d_sent, f_sent,
):
    blk, uly = lax.axis_index("blk"), lax.axis_index("uly")
    hi, x, z = blk // 16, (blk // 4) % 4, blk % 4
    me = hi * 4 + uly
    role = lax.rem(hi + uly // 2, 2)

    def column(member):
        return ((member // 4) * 16 + x * 4 + z, member % 4)

    def along_x(step):
        return (hi * 16 + lax.rem(x + step, 4) * 4 + z, uly)

    def along_z(step):
        return (hi * 16 + x * 4 + lax.rem(z + step, 4), uly)

    def remote(src, dst, sent, arrived, to):
        return pltpu.make_async_remote_copy(src, dst, sent, arrived, device_id=to, device_id_type=MESH)

    def wait_for(ref, sem):
        pltpu.make_async_copy(ref, ref, sem).wait()

    barrier = pltpu.get_barrier_semaphore()
    for step in range(1, 8):
        pl.semaphore_signal(barrier, inc=1, device_id=column(lax.rem(me + step, 8)), device_id_type=MESH)
    for step in (1, 2, 3):
        pl.semaphore_signal(barrier, inc=1, device_id=along_z(step), device_id_type=MESH)
    for step in (1, 3):
        pl.semaphore_signal(barrier, inc=1, device_id=along_x(step), device_id_type=MESH)

    def unit_lanes(unit, group=None):
        first, count = UNITS[unit]
        if group is None:
            return pl.ds(first * HD, count * HD)
        return pl.ds(pl.multiple_of(group * WIDTH + first * HD, HD), count * HD)

    def y_start(unit):
        lanes = unit_lanes(unit)
        rows = pl.ds(pl.multiple_of(hi * SHARD, SHARD), SHARD)
        cond = (
            (q_hbm.at[:, lanes], qkv.at[0, rows, lanes]),
            (kv_hbm.at[:, :, lanes], qkv.at[pl.ds(1, 2), rows, lanes]))
        piece = qkv.at[:, pl.ds(pl.multiple_of(me * PIECE, PIECE), PIECE), lanes]

        @pl.when(role == 0)
        def _():
            for src, dst in cond:
                pltpu.make_async_copy(src, dst, y_sem.at[unit]).start()

        @pl.when(role == 1)
        def _():
            for src, dst in cond:
                remote(src, dst, y_sent, y_sem.at[unit], column((uly // 2) * 4 + uly)).start()
            pltpu.make_async_copy(qkv_hbm.at[:, :, unit_lanes(unit, uly)], piece, y_sem.at[unit]).start()

        for group in range(4):
            owner = (1 - group // 2) * 4 + group

            @pl.when(me != owner)
            def _():
                remote(qkv_hbm.at[:, :, unit_lanes(unit, group)], piece, y_sent, y_sem.at[unit], column(owner)).start()

    def y_wait(unit):
        wait_for(qkv.at[:, slot_rows(0), unit_lanes(unit)], y_sem.at[unit])

    def y_settle():
        @pl.when(role == 0)
        def _():
            wait_for(qkv.at[:, pl.ds(0, SHARD), :], y_sent)

        @pl.when(role == 1)
        def _():
            wait_for(qkv.at[:, pl.ds(0, PAIR - PIECE), :], y_sent)

    def gathered(kind, head, rows):
        return qkv.at[0 if kind == 0 else pl.ds(1, 2), rows, head_lanes(head)]

    def gather(kind, head, order):
        for step, slot, row in ((1, 1, 0), (3, 3, SHARD)):
            if order == 0:
                src, dst = slot_rows(0), slot_rows(slot)
            else:
                src, dst = pl.ds(slot * PAIR + row, SHARD), pl.ds(2 * PAIR + row, SHARD)
            remote(
                gathered(kind, head, src), gathered(kind, head, dst), g_sent.at[kind], g_sem.at[head, kind, order],
                along_z(step) if kind == 0 else along_x(step)).start()

    def gather_wait(kind, head, order):
        wait_for(gathered(kind, head, pl.ds(0, (2 - order) * PAIR)), g_sem.at[head, kind, order])

    def direct(slot):
        to = along_z(STEPS[slot])
        into = STEPS[slot] - 1
        remote(o_send.at[LAST, :, slot_rows(slot)], o_recv.at[into], d_sent.at[0], d_sem.at[0], to).start()
        remote(st_send.at[LAST, slot], st_recv.at[into], d_sent.at[1], d_sem.at[1], to).start()

    def hand_over(head, stage_of):
        for side, step in ((0, 1), (1, 3)):
            if stage_of == 0:
                data = (o_send.at[head, pl.ds(side * HALF, HALF), slot_rows(2)], o_half_in.at[head, side])
                note = (st_send.at[head, 2], st_half_in.at[head, side])
            else:
                data = (o_full.at[head, side], o_full_in.at[head, side])
                note = (st_full.at[head, side], st_full_in.at[head, side])
            for i, (src, dst) in enumerate((data, note)):
                remote(src, dst, o_sent.at[stage_of, i], o_sem.at[head, stage_of, i], along_z(step)).start()

    def give_back(first, count):
        src_lanes = pl.ds(first * HD, count * HD)
        dst_lanes = pl.ds(pl.multiple_of(uly * WIDTH + first * HD, HD), count * HD)

        def refs(target):
            rows = pl.ds(pl.multiple_of(target * PIECE, PIECE), PIECE)
            return stage.at[rows, src_lanes], tokens.at[role, :, dst_lanes]

        for step in range(1, 8):
            target = lax.rem(me + step, 8)
            src, dst = refs(target)
            remote(src, dst, f_sent, f_sem, column(target)).start()
        src, dst = refs(me)
        pltpu.make_async_copy(src, dst, f_sem).start()

    def prepare():
        lane = lax.broadcasted_iota(jnp.int32, (SHARD, HD), 1)
        row = lax.broadcasted_iota(jnp.int32, (SHARD, HD), 0)
        for slot in range(4):
            for half in range(2):
                present = valid_ref[half * 16 + lax.rem(x + 4 - slot, 4) * 4 + z]
                block = jnp.where((row >= present) & (lane == 0), UNUSABLE, 0.0)
                bias[pl.ds(slot * PAIR + half * SHARD, SHARD), :] = block.astype(jnp.bfloat16)
        ones[...] = jnp.where(
            lax.broadcasted_iota(jnp.int32, (TILE, HD), 1) == 0, 1.0, 0.0).astype(jnp.bfloat16)
        vt[pl.ds(HD, 16), :] = jnp.ones((16, ALL), jnp.bfloat16)

    def transpose_values(head, slots):
        rows = lax.broadcasted_iota(jnp.int32, (HD, HD), 0)
        lanes = lax.broadcasted_iota(jnp.int32, (HD, HD), 1)
        eye = (rows == lanes).astype(jnp.bfloat16)
        for slot in slots:
            vt[pl.ds(0, HD), slot_rows(slot)] = lax.dot_general(
                eye, qkv[2, slot_rows(slot), head_lanes(head)], NT,
                preferred_element_type=jnp.float32).astype(jnp.bfloat16)

    def attend_slots(head, slots, combine, store):
        buffers = (scores_even, scores_odd)
        starts = [i * TILE for i in (3, 4, 5, 2, 1, 0)]

        def scored(i, k):
            queries = jnp.concatenate([qkv[0, pl.ds(starts[i], TILE), head_lanes(head)], ones[...]], axis=1)
            keys = jnp.concatenate([qkv[1, slot_rows(slots[k]), head_lanes(head)], bias[slot_rows(slots[k]), :]], axis=1)
            part = lax.dot_general(keys, queries, NT, preferred_element_type=jnp.float32)
            buffers[i % 2][slot_rows(k), :] = part
            return jnp.max(part.reshape(PAIR // 8, 8, TILE), axis=0)

        def weighted(i, k, top):
            weights = jnp.exp2((buffers[i % 2][slot_rows(k), :] - top) * SCALE).astype(jnp.bfloat16)
            return jnp.dot(vt[:, slot_rows(slots[k])], weights, preferred_element_type=jnp.float32)

        def whole(parts):
            return jnp.max(functools.reduce(jnp.maximum, parts), axis=0, keepdims=True)

        top = whole([scored(0, k) for k in range(len(slots))])
        for i, start in enumerate(starts):
            lanes = pl.ds(start, TILE)
            top = combine(lanes, top)
            total, next_tops = None, []
            for k in range(len(slots)):
                if i + 1 < len(starts):
                    next_tops.append(scored(i + 1, k))
                part = weighted(i, k, top)
                total = part if total is None else total + part
            store(i, lanes, top, total)
            if next_tops:
                top = whole(next_tops)

    def packed(top, total):
        rows = [row[:, i * HD:(i + 1) * HD] for row in (top, total) for i in range(3)]
        return jnp.concatenate(rows + [jnp.zeros((2, HD), jnp.float32)], axis=0)

    def unpacked(block):
        return tuple(
            jnp.concatenate([block[k + i:k + i + 1] for i in range(3)], axis=1) for k in (0, 3))

    def near_keys(head):
        transpose_values(head, (0, 1, 3))

        def store(i, lanes, top, total):
            partial[:, lanes] = total
            tops[:, lanes] = top

        attend_slots(head, (0, 1, 3), lambda lanes, top: top, store)

    def far_keys(head):
        transpose_values(head, (2,))

        def combine(lanes, top):
            return jnp.maximum(top, tops[:, lanes])

        def store(i, lanes, top, total):
            total = total + partial[:, lanes] * jnp.exp2((tops[:, lanes] - top) * SCALE)
            o_send[head, :, lanes] = total[:HD].astype(jnp.bfloat16)
            stats[pl.ds(0, 1), lanes] = top
            stats[pl.ds(1, 1), lanes] = total[HD:HD + 1]
            slot = {1: 2, 2: 3, 4: 1, 5: 0}.get(i)
            if slot is not None:
                st_send[head, slot] = packed(
                    stats[pl.ds(0, 1), slot_rows(slot)], stats[pl.ds(1, 1), slot_rows(slot)])
            if slot == 2:
                @pl.when(head < LAST)
                def _():
                    hand_over(head, 0)
            if slot:
                @pl.when(head == LAST)
                def _():
                    direct(slot)

        attend_slots(head, (2,), combine, store)

    def pass_on(head):
        wait_for(o_half_in.at[head], o_sem.at[head, 0, 0])
        wait_for(st_half_in.at[head], o_sem.at[head, 0, 1])
        for side, slot in ((0, 3), (1, 1)):
            own_top, own_sum = unpacked(st_send[head, slot])
            in_top, in_sum = unpacked(st_half_in[head, side])
            top = jnp.maximum(own_top, in_top)
            own_factor, in_factor = jnp.exp2((own_top - top) * SCALE), jnp.exp2((in_top - top) * SCALE)
            for half in range(2):
                rows = pl.ds(half * HALF, HALF)
                block = o_send[head, rows, slot_rows(slot)].astype(jnp.float32) * own_factor
                if half == side:
                    block = block + o_half_in[head, side].astype(jnp.float32) * in_factor
                o_full[head, side, rows] = block.astype(jnp.bfloat16)
            total = own_sum * own_factor
            if side == 0:
                total = total + in_sum * in_factor
            st_full[head, side] = packed(top, total)
        hand_over(head, 1)

    def merge(head):
        if isinstance(head, int) and head == LAST:
            wait_for(o_recv, d_sem.at[0])
            wait_for(st_recv, d_sem.at[1])
            arrived = [(o_recv[i], st_recv[i]) for i in range(3)]
        else:
            wait_for(o_full_in.at[head], o_sem.at[head, 1, 0])
            wait_for(st_full_in.at[head], o_sem.at[head, 1, 1])
            arrived = [(o_full_in[head, side], st_full_in[head, side]) for side in range(2)]
        arrived.append((o_send[head, :, slot_rows(0)], st_send[head, 0]))
        pairs = [unpacked(block) for _, block in arrived]
        top = functools.reduce(jnp.maximum, [pair[0] for pair in pairs])
        factors = [jnp.exp2((pair[0] - top) * SCALE) for pair in pairs]
        denominator = sum(f * pair[1] for f, pair in zip(factors, pairs))
        numerator = sum(f * block.astype(jnp.float32) for f, (block, _) in zip(factors, arrived))
        stage[:, head_lanes(head)] = (numerator / denominator).T.astype(jnp.bfloat16)

    def spread(head):
        for kind in range(2):
            gather(kind, head, 0)

    def relay(head):
        for kind in range(2):
            gather_wait(kind, head, 0)
            gather(kind, head, 1)

    def head_step(head, _):
        gather_wait(0, head, 1)
        near_keys(head)

        @pl.when(head < LAST)
        def _():
            relay(head + 1)

        @pl.when(head >= 1)
        def _():
            pass_on(head - 1)

        gather_wait(1, head, 1)
        far_keys(head)

        @pl.when(head == 0)
        def _():
            y_wait(3)

        @pl.when(head + 3 < HEADS)
        def _():
            spread(head + 3)

        @pl.when(head >= 2)
        def _():
            merge(head - 2)

        return 0

    pl.semaphore_wait(barrier, 12)
    y_start(0)
    y_start(1)
    prepare()
    y_wait(0)
    spread(0)
    y_start(2)
    y_wait(1)
    spread(1)
    y_start(3)
    relay(0)
    y_wait(2)
    spread(2)
    lax.fori_loop(0, HEADS, head_step, 0)
    merge(LAST - 1)
    give_back(0, LAST)
    y_settle()
    wait_for(qkv.at[0, pl.ds(0, 3 * PAIR), :], g_sent.at[0])
    wait_for(qkv.at[pl.ds(1, 2), pl.ds(0, 3 * PAIR), :], g_sent.at[1])
    for i, (data, note) in enumerate(((o_half_in, st_half_in), (o_full, st_full))):
        wait_for(data, o_sent.at[i, 0])
        wait_for(note, o_sent.at[i, 1])
    merge(LAST)
    give_back(LAST, 1)
    wait_for(o_recv, d_sent.at[0])
    wait_for(st_recv, d_sent.at[1])
    lanes = lax.broadcasted_iota(jnp.int32, (PIECE, PIECE), 1)
    rows = lax.broadcasted_iota(jnp.int32, (PIECE, PIECE), 0)
    chosen = jnp.where((rows == lanes) & (refresh_ref[...] == 1), 1.0, 0.0).astype(jnp.bfloat16)
    renew = jnp.dot(chosen, jnp.ones((PIECE, HD), jnp.bfloat16), preferred_element_type=jnp.float32) > 0.5
    wait_for(stage.at[pl.ds(0, PAIR - PIECE), :], f_sent)
    wait_for(tokens, f_sem)
    for block in range(4 * HEADS):
        columns = pl.ds(block * HD, HD)
        kept = cache_ref[:, columns].astype(jnp.float32)
        kept = jnp.where(renew, tokens[1, :, columns].astype(jnp.float32), kept)
        cache_out[:, columns] = kept.astype(jnp.bfloat16)
        guided = kept + GUIDANCE * (tokens[0, :, columns].astype(jnp.float32) - kept)
        guided_out[:, columns] = guided.astype(jnp.bfloat16)


def on_device(cond_query, cond_kv, uncond_qkv, uncond_cache, refresh, valid):
    any_space = pl.BlockSpec(memory_space=pl.ANY)
    vmem = pl.BlockSpec(memory_space=pltpu.VMEM)
    dma = pltpu.SemaphoreType.DMA
    bf16, f32 = jnp.bfloat16, jnp.float32
    result = jax.ShapeDtypeStruct((PIECE, 4 * WIDTH), bf16)
    return pl.pallas_call(
        kernel,
        out_shape=(result, result),
        in_specs=[pl.BlockSpec(memory_space=pltpu.SMEM), any_space, any_space, any_space, vmem, vmem],
        out_specs=(vmem, vmem),
        scratch_shapes=[
            pltpu.VMEM((3, ALL, WIDTH), bf16),
            pltpu.VMEM((HD + 16, ALL), bf16),
            pltpu.VMEM((ALL, HD), bf16),
            pltpu.VMEM((TILE, HD), bf16),
            pltpu.VMEM((3 * PAIR, TILE), f32),
            pltpu.VMEM((3 * PAIR, TILE), f32),
            pltpu.VMEM((HD + 16, ALL), f32),
            pltpu.VMEM((1, ALL), f32),
            pltpu.VMEM((8, ALL), f32),
            pltpu.VMEM((HEADS, HD, ALL), bf16),
            pltpu.VMEM((HEADS, 4, 8, HD), f32),
            pltpu.VMEM((LAST, 2, HALF, PAIR), bf16),
            pltpu.VMEM((LAST, 2, 8, HD), f32),
            pltpu.VMEM((LAST, 2, HD, PAIR), bf16),
            pltpu.VMEM((LAST, 2, HD, PAIR), bf16),
            pltpu.VMEM((LAST, 2, 8, HD), f32),
            pltpu.VMEM((LAST, 2, 8, HD), f32),
            pltpu.VMEM((3, HD, PAIR), bf16),
            pltpu.VMEM((3, 8, HD), f32),
            pltpu.VMEM((PAIR, WIDTH), bf16),
            pltpu.VMEM((2, PIECE, 4 * WIDTH), bf16),
            dma((len(UNITS),)), dma((HEADS, 2, 2)), dma((LAST, 2, 2)), dma((2,)), dma,
            dma, dma((2,)), dma((2, 2)), dma((2,)), dma,
        ],
        compiler_params=pltpu.CompilerParams(
            collective_id=0, has_side_effects=True, vmem_limit_bytes=60 << 20),
    )(valid, cond_query, cond_kv, uncond_qkv, uncond_cache, refresh.reshape(1, PIECE))


def solution(mesh):
    placed = (
        P("blk", "uly"),
        P(None, "blk", "uly"),
        P(None, ("blk", "uly"), None),
        P(("blk", "uly"), None),
        P(("blk", "uly")),
        P(),
    )
    return jax.shard_map(
        on_device,
        mesh=mesh,
        in_specs=placed,
        out_specs=(P(("blk", "uly"), None), P(("blk", "uly"), None)),
        check_vma=False,
    )
```

```python
import functools

import jax
import jax.numpy as jnp
from jax import lax
from jax.experimental import pallas as pl
from jax.experimental.pallas import tpu as pltpu
from jax.sharding import PartitionSpec as P

HD = 128
GUIDANCE = 5.0
MESH = pl.DeviceIdType.MESH
LOG2E = 1.4426950408889634
SCALE = LOG2E * HD ** (-0.5)
UNUSABLE = -1e30

HALF = HD // 2
HEADS = 5
LAST = HEADS - 1
WIDTH = HEADS * HD
UNITS = ((1, 1, 0, 1), (2, 1, 0, 1), (0, 1, 0, 1), (0, 3, 1, 1), (0, 3, 2, 1), (0, 3, 3, 2))
SHARD = 192
PIECE = 48
PAIR = 2 * SHARD
ALL = 4 * PAIR
TILE = 256
NT = (((1,), (1,)), ((), ()))
STEPS = (0, 3, 2, 1)


def slot_rows(slot):
    return pl.ds(slot * PAIR, PAIR)


def head_lanes(head):
    return pl.ds(pl.multiple_of(head * HD, HD), HD)


def kernel(
    valid_ref, q_hbm, kv_hbm, qkv_hbm, cache_ref, refresh_ref, guided_out, cache_out,
    qkv, vt, bias, ones, scores_even, scores_odd, partial, tops, stats,
    o_send, st_send, o_half_in, st_half_in, o_full, o_full_in, st_full, st_full_in, o_recv, st_recv, stage, tokens,
    y_sem, g_sem, o_sem, d_sem, f_sem, y_sent, g_sent, o_sent, d_sent, f_sent,
):
    blk, uly = lax.axis_index("blk"), lax.axis_index("uly")
    hi, x, z = blk // 16, (blk // 4) % 4, blk % 4
    me = hi * 4 + uly
    role = lax.rem(hi + uly // 2, 2)

    def column(member):
        return ((member // 4) * 16 + x * 4 + z, member % 4)

    def along_x(step):
        return (hi * 16 + lax.rem(x + step, 4) * 4 + z, uly)

    def along_z(step):
        return (hi * 16 + x * 4 + lax.rem(z + step, 4), uly)

    def remote(src, dst, sent, arrived, to):
        return pltpu.make_async_remote_copy(src, dst, sent, arrived, device_id=to, device_id_type=MESH)

    def wait_for(ref, sem):
        pltpu.make_async_copy(ref, ref, sem).wait()

    barrier = pltpu.get_barrier_semaphore()
    for step in range(1, 8):
        pl.semaphore_signal(barrier, inc=1, device_id=column(lax.rem(me + step, 8)), device_id_type=MESH)
    for step in (1, 2, 3):
        pl.semaphore_signal(barrier, inc=1, device_id=along_z(step), device_id_type=MESH)
    for step in (1, 3):
        pl.semaphore_signal(barrier, inc=1, device_id=along_x(step), device_id_type=MESH)

    def unit_lanes(unit, group=None):
        first, count = UNITS[unit][2:]
        if group is None:
            return pl.ds(first * HD, count * HD)
        return pl.ds(pl.multiple_of(group * WIDTH + first * HD, HD), count * HD)

    def y_start(unit):
        lanes = unit_lanes(unit)
        rows = pl.ds(pl.multiple_of(hi * SHARD, SHARD), SHARD)
        first, count = UNITS[unit][:2]
        cond = []
        if first == 0:
            cond.append((q_hbm.at[:, lanes], qkv.at[0, rows, lanes]))
        if first + count > 1:
            low = max(first, 1)
            span = first + count - low
            cond.append((kv_hbm.at[pl.ds(low - 1, span), :, lanes], qkv.at[pl.ds(low, span), rows, lanes]))
        arrays = pl.ds(first, count)
        piece = qkv.at[arrays, pl.ds(pl.multiple_of(me * PIECE, PIECE), PIECE), lanes]

        @pl.when(role == 0)
        def _():
            for src, dst in cond:
                pltpu.make_async_copy(src, dst, y_sem.at[unit]).start()

        @pl.when(role == 1)
        def _():
            for src, dst in cond:
                remote(src, dst, y_sent, y_sem.at[unit], column((uly // 2) * 4 + uly)).start()
            pltpu.make_async_copy(qkv_hbm.at[arrays, :, unit_lanes(unit, uly)], piece, y_sem.at[unit]).start()

        for group in range(4):
            owner = (1 - group // 2) * 4 + group

            @pl.when(me != owner)
            def _():
                remote(
                    qkv_hbm.at[arrays, :, unit_lanes(unit, group)], piece, y_sent, y_sem.at[unit],
                    column(owner)).start()

    def y_wait(unit):
        wait_for(qkv.at[pl.ds(*UNITS[unit][:2]), slot_rows(0), unit_lanes(unit)], y_sem.at[unit])

    def y_settle():
        @pl.when(role == 0)
        def _():
            wait_for(qkv.at[:, pl.ds(0, SHARD), :], y_sent)

        @pl.when(role == 1)
        def _():
            wait_for(qkv.at[:, pl.ds(0, PAIR - PIECE), :], y_sent)

    def gathered(kind, head, rows, arrays=None):
        return qkv.at[0 if kind == 0 else pl.ds(1, 2) if arrays is None else arrays, rows, head_lanes(head)]

    def gather(kind, head, order, arrays=None):
        for step, slot, row in ((1, 1, 0), (3, 3, SHARD)):
            if order == 0:
                src, dst = slot_rows(0), slot_rows(slot)
            else:
                src, dst = pl.ds(slot * PAIR + row, SHARD), pl.ds(2 * PAIR + row, SHARD)
            remote(
                gathered(kind, head, src, arrays), gathered(kind, head, dst, arrays), g_sent.at[kind],
                g_sem.at[head, kind, order], along_z(step) if kind == 0 else along_x(step)).start()

    def gather_wait(kind, head, order):
        wait_for(gathered(kind, head, pl.ds(0, (2 - order) * PAIR)), g_sem.at[head, kind, order])

    def direct(slot):
        to = along_z(STEPS[slot])
        into = STEPS[slot] - 1
        remote(o_send.at[LAST, :, slot_rows(slot)], o_recv.at[into], d_sent.at[0], d_sem.at[0], to).start()
        remote(st_send.at[LAST, slot], st_recv.at[into], d_sent.at[1], d_sem.at[1], to).start()

    def hand_over(head, stage_of):
        for side, step in ((0, 1), (1, 3)):
            if stage_of == 0:
                data = (o_send.at[head, pl.ds(side * HALF, HALF), slot_rows(2)], o_half_in.at[head, side])
                note = (st_send.at[head, 2], st_half_in.at[head, side])
            else:
                data = (o_full.at[head, side], o_full_in.at[head, side])
                note = (st_full.at[head, side], st_full_in.at[head, side])
            for i, (src, dst) in enumerate((data, note)):
                remote(src, dst, o_sent.at[stage_of, i], o_sem.at[head, stage_of, i], along_z(step)).start()

    def give_back(first, count):
        src_lanes = pl.ds(first * HD, count * HD)
        dst_lanes = pl.ds(pl.multiple_of(uly * WIDTH + first * HD, HD), count * HD)

        def refs(target):
            rows = pl.ds(pl.multiple_of(target * PIECE, PIECE), PIECE)
            return stage.at[rows, src_lanes], tokens.at[role, :, dst_lanes]

        for step in range(1, 8):
            target = lax.rem(me + step, 8)
            src, dst = refs(target)
            remote(src, dst, f_sent, f_sem, column(target)).start()
        src, dst = refs(me)
        pltpu.make_async_copy(src, dst, f_sem).start()

    def prepare():
        lane = lax.broadcasted_iota(jnp.int32, (SHARD, HD), 1)
        row = lax.broadcasted_iota(jnp.int32, (SHARD, HD), 0)
        for slot in range(4):
            for half in range(2):
                present = valid_ref[half * 16 + lax.rem(x + 4 - slot, 4) * 4 + z]
                block = jnp.where((row >= present) & (lane == 0), UNUSABLE, 0.0)
                bias[pl.ds(slot * PAIR + half * SHARD, SHARD), :] = block.astype(jnp.bfloat16)
        ones[...] = jnp.where(
            lax.broadcasted_iota(jnp.int32, (TILE, HD), 1) == 0, 1.0, 0.0).astype(jnp.bfloat16)
        vt[pl.ds(HD, 16), :] = jnp.ones((16, ALL), jnp.bfloat16)

    def transpose_values(head, slots):
        rows = lax.broadcasted_iota(jnp.int32, (HD, HD), 0)
        lanes = lax.broadcasted_iota(jnp.int32, (HD, HD), 1)
        eye = (rows == lanes).astype(jnp.bfloat16)
        for slot in slots:
            vt[pl.ds(0, HD), slot_rows(slot)] = lax.dot_general(
                eye, qkv[2, slot_rows(slot), head_lanes(head)], NT,
                preferred_element_type=jnp.float32).astype(jnp.bfloat16)

    def attend_slots(head, slots, combine, store):
        buffers = (scores_even, scores_odd)
        starts = [i * TILE for i in (3, 4, 5, 2, 1, 0)]

        def scored(i, k):
            queries = jnp.concatenate([qkv[0, pl.ds(starts[i], TILE), head_lanes(head)], ones[...]], axis=1)
            keys = jnp.concatenate([qkv[1, slot_rows(slots[k]), head_lanes(head)], bias[slot_rows(slots[k]), :]], axis=1)
            part = lax.dot_general(keys, queries, NT, preferred_element_type=jnp.float32)
            buffers[i % 2][slot_rows(k), :] = part
            return jnp.max(part.reshape(PAIR // 8, 8, TILE), axis=0)

        def weighted(i, k, top):
            weights = jnp.exp2((buffers[i % 2][slot_rows(k), :] - top) * SCALE).astype(jnp.bfloat16)
            return jnp.dot(vt[:, slot_rows(slots[k])], weights, preferred_element_type=jnp.float32)

        def whole(parts):
            return jnp.max(functools.reduce(jnp.maximum, parts), axis=0, keepdims=True)

        top = whole([scored(0, k) for k in range(len(slots))])
        for i, start in enumerate(starts):
            lanes = pl.ds(start, TILE)
            top = combine(lanes, top)
            total, next_tops = None, []
            for k in range(len(slots)):
                if i + 1 < len(starts):
                    next_tops.append(scored(i + 1, k))
                part = weighted(i, k, top)
                total = part if total is None else total + part
            store(i, lanes, top, total)
            if next_tops:
                top = whole(next_tops)

    def packed(top, total):
        rows = [row[:, i * HD:(i + 1) * HD] for row in (top, total) for i in range(3)]
        return jnp.concatenate(rows + [jnp.zeros((2, HD), jnp.float32)], axis=0)

    def unpacked(block):
        return tuple(
            jnp.concatenate([block[k + i:k + i + 1] for i in range(3)], axis=1) for k in (0, 3))

    def near_keys(head):
        transpose_values(head, (0, 1, 3))

        def store(i, lanes, top, total):
            partial[:, lanes] = total
            tops[:, lanes] = top

        attend_slots(head, (0, 1, 3), lambda lanes, top: top, store)

    def far_keys(head):
        transpose_values(head, (2,))

        def combine(lanes, top):
            return jnp.maximum(top, tops[:, lanes])

        def store(i, lanes, top, total):
            total = total + partial[:, lanes] * jnp.exp2((tops[:, lanes] - top) * SCALE)
            o_send[head, :, lanes] = total[:HD].astype(jnp.bfloat16)
            stats[pl.ds(0, 1), lanes] = top
            stats[pl.ds(1, 1), lanes] = total[HD:HD + 1]
            slot = {1: 2, 2: 3, 4: 1, 5: 0}.get(i)
            if slot is not None:
                st_send[head, slot] = packed(
                    stats[pl.ds(0, 1), slot_rows(slot)], stats[pl.ds(1, 1), slot_rows(slot)])
            if slot == 2:
                @pl.when(head < LAST)
                def _():
                    hand_over(head, 0)
            if slot:
                @pl.when(head == LAST)
                def _():
                    direct(slot)

        attend_slots(head, (2,), combine, store)

    def pass_on(head):
        wait_for(o_half_in.at[head], o_sem.at[head, 0, 0])
        wait_for(st_half_in.at[head], o_sem.at[head, 0, 1])
        for side, slot in ((0, 3), (1, 1)):
            own_top, own_sum = unpacked(st_send[head, slot])
            in_top, in_sum = unpacked(st_half_in[head, side])
            top = jnp.maximum(own_top, in_top)
            own_factor, in_factor = jnp.exp2((own_top - top) * SCALE), jnp.exp2((in_top - top) * SCALE)
            for half in range(2):
                rows = pl.ds(half * HALF, HALF)
                block = o_send[head, rows, slot_rows(slot)].astype(jnp.float32) * own_factor
                if half == side:
                    block = block + o_half_in[head, side].astype(jnp.float32) * in_factor
                o_full[head, side, rows] = block.astype(jnp.bfloat16)
            total = own_sum * own_factor
            if side == 0:
                total = total + in_sum * in_factor
            st_full[head, side] = packed(top, total)
        hand_over(head, 1)

    def merge(head):
        if isinstance(head, int) and head == LAST:
            wait_for(o_recv, d_sem.at[0])
            wait_for(st_recv, d_sem.at[1])
            arrived = [(o_recv[i], st_recv[i]) for i in range(3)]
        else:
            wait_for(o_full_in.at[head], o_sem.at[head, 1, 0])
            wait_for(st_full_in.at[head], o_sem.at[head, 1, 1])
            arrived = [(o_full_in[head, side], st_full_in[head, side]) for side in range(2)]
        arrived.append((o_send[head, :, slot_rows(0)], st_send[head, 0]))
        pairs = [unpacked(block) for _, block in arrived]
        top = functools.reduce(jnp.maximum, [pair[0] for pair in pairs])
        factors = [jnp.exp2((pair[0] - top) * SCALE) for pair in pairs]
        denominator = sum(f * pair[1] for f, pair in zip(factors, pairs))
        numerator = sum(f * block.astype(jnp.float32) for f, (block, _) in zip(factors, arrived))
        stage[:, head_lanes(head)] = (numerator / denominator).T.astype(jnp.bfloat16)

    def spread(head):
        for kind in range(2):
            gather(kind, head, 0)

    def relay(head):
        for kind in range(2):
            gather_wait(kind, head, 0)
            gather(kind, head, 1)

    def head_step(head, _):
        gather_wait(0, head, 1)
        near_keys(head)

        @pl.when(head < LAST)
        def _():
            relay(head + 1)

        @pl.when(head >= 1)
        def _():
            pass_on(head - 1)

        gather_wait(1, head, 1)
        far_keys(head)

        @pl.when(head == 0)
        def _():
            y_wait(5)

        @pl.when(head + 3 < HEADS)
        def _():
            spread(head + 3)

        @pl.when(head >= 2)
        def _():
            merge(head - 2)

        @pl.when(head == 3)
        def _():
            give_back(0, 2)

        @pl.when(head == 4)
        def _():
            give_back(2, 1)

        return 0

    pl.semaphore_wait(barrier, 12)
    for unit in range(len(UNITS)):
        y_start(unit)
    prepare()
    y_wait(0)
    gather(1, 0, 0, 1)
    y_wait(1)
    gather(1, 0, 0, 2)
    y_wait(2)
    gather(0, 0, 0)
    y_wait(3)
    spread(1)
    relay(0)
    y_wait(4)
    spread(2)
    lax.fori_loop(0, HEADS, head_step, 0)
    merge(LAST - 1)
    give_back(3, 1)
    y_settle()
    wait_for(qkv.at[0, pl.ds(0, 3 * PAIR), :], g_sent.at[0])
    wait_for(qkv.at[pl.ds(1, 2), pl.ds(0, 3 * PAIR), :], g_sent.at[1])
    for i, (data, note) in enumerate(((o_half_in, st_half_in), (o_full, st_full))):
        wait_for(data, o_sent.at[i, 0])
        wait_for(note, o_sent.at[i, 1])
    merge(LAST)
    give_back(LAST, 1)
    wait_for(o_recv, d_sent.at[0])
    wait_for(st_recv, d_sent.at[1])
    lanes = lax.broadcasted_iota(jnp.int32, (PIECE, PIECE), 1)
    rows = lax.broadcasted_iota(jnp.int32, (PIECE, PIECE), 0)
    chosen = jnp.where((rows == lanes) & (refresh_ref[...] == 1), 1.0, 0.0).astype(jnp.bfloat16)
    renew = jnp.dot(chosen, jnp.ones((PIECE, HD), jnp.bfloat16), preferred_element_type=jnp.float32) > 0.5
    wait_for(stage.at[pl.ds(0, PAIR - PIECE), :], f_sent)
    wait_for(tokens, f_sem)
    for block in range(4 * HEADS):
        columns = pl.ds(block * HD, HD)
        kept = cache_ref[:, columns].astype(jnp.float32)
        kept = jnp.where(renew, tokens[1, :, columns].astype(jnp.float32), kept)
        cache_out[:, columns] = kept.astype(jnp.bfloat16)
        guided = kept + GUIDANCE * (tokens[0, :, columns].astype(jnp.float32) - kept)
        guided_out[:, columns] = guided.astype(jnp.bfloat16)


def on_device(cond_query, cond_kv, uncond_qkv, uncond_cache, refresh, valid):
    any_space = pl.BlockSpec(memory_space=pl.ANY)
    vmem = pl.BlockSpec(memory_space=pltpu.VMEM)
    dma = pltpu.SemaphoreType.DMA
    bf16, f32 = jnp.bfloat16, jnp.float32
    result = jax.ShapeDtypeStruct((PIECE, 4 * WIDTH), bf16)
    return pl.pallas_call(
        kernel,
        out_shape=(result, result),
        in_specs=[pl.BlockSpec(memory_space=pltpu.SMEM), any_space, any_space, any_space, vmem, vmem],
        out_specs=(vmem, vmem),
        scratch_shapes=[
            pltpu.VMEM((3, ALL, WIDTH), bf16),
            pltpu.VMEM((HD + 16, ALL), bf16),
            pltpu.VMEM((ALL, HD), bf16),
            pltpu.VMEM((TILE, HD), bf16),
            pltpu.VMEM((3 * PAIR, TILE), f32),
            pltpu.VMEM((3 * PAIR, TILE), f32),
            pltpu.VMEM((HD + 16, ALL), f32),
            pltpu.VMEM((1, ALL), f32),
            pltpu.VMEM((8, ALL), f32),
            pltpu.VMEM((HEADS, HD, ALL), bf16),
            pltpu.VMEM((HEADS, 4, 8, HD), f32),
            pltpu.VMEM((LAST, 2, HALF, PAIR), bf16),
            pltpu.VMEM((LAST, 2, 8, HD), f32),
            pltpu.VMEM((LAST, 2, HD, PAIR), bf16),
            pltpu.VMEM((LAST, 2, HD, PAIR), bf16),
            pltpu.VMEM((LAST, 2, 8, HD), f32),
            pltpu.VMEM((LAST, 2, 8, HD), f32),
            pltpu.VMEM((3, HD, PAIR), bf16),
            pltpu.VMEM((3, 8, HD), f32),
            pltpu.VMEM((PAIR, WIDTH), bf16),
            pltpu.VMEM((2, PIECE, 4 * WIDTH), bf16),
            dma((len(UNITS),)), dma((HEADS, 2, 2)), dma((LAST, 2, 2)), dma((2,)), dma,
            dma, dma((2,)), dma((2, 2)), dma((2,)), dma,
        ],
        compiler_params=pltpu.CompilerParams(
            collective_id=0, has_side_effects=True, vmem_limit_bytes=60 << 20),
    )(valid, cond_query, cond_kv, uncond_qkv, uncond_cache, refresh.reshape(1, PIECE))


def solution(mesh):
    placed = (
        P("blk", "uly"),
        P(None, "blk", "uly"),
        P(None, ("blk", "uly"), None),
        P(("blk", "uly"), None),
        P(("blk", "uly")),
        P(),
    )
    return jax.shard_map(
        on_device,
        mesh=mesh,
        in_specs=placed,
        out_specs=(P(("blk", "uly"), None), P(("blk", "uly"), None)),
        check_vma=False,
    )
```

```python
import functools

import jax
import jax.numpy as jnp
from jax import lax
from jax.experimental import pallas as pl
from jax.experimental.pallas import tpu as pltpu
from jax.sharding import PartitionSpec as P

HD = 128
GUIDANCE = 5.0
MESH = pl.DeviceIdType.MESH
LOG2E = 1.4426950408889634
SCALE = LOG2E * HD ** (-0.5)
UNUSABLE = -1e30

HALF = HD // 2
HEADS = 5
LAST = HEADS - 1
WIDTH = HEADS * HD
UNITS = ((1, 1, 0, 1), (2, 1, 0, 1), (0, 1, 0, 1), (0, 3, 1, 1), (0, 3, 2, 1), (0, 3, 3, 2))
RETURNS = ((0, 2), (2, 1), (3, 1), (4, 1))
SHARD = 192
PIECE = 48
PAIR = 2 * SHARD
ALL = 4 * PAIR
TILE = 256
NT = (((1,), (1,)), ((), ()))
STEPS = (0, 3, 2, 1)


def slot_rows(slot):
    return pl.ds(slot * PAIR, PAIR)


def head_lanes(head):
    return pl.ds(pl.multiple_of(head * HD, HD), HD)


def kernel(
    valid_ref, q_hbm, kv_hbm, qkv_hbm, cache_ref, refresh_ref, guided_out, cache_out,
    qkv, vt, bias, ones, scores_even, scores_odd, partial, tops, stats,
    o_send, st_send, o_half_in, st_half_in, o_full, o_full_in, st_full, st_full_in, o_recv, st_recv, stage, tokens,
    y_sem, g_sem, o_sem, d_sem, f_sem, y_sent, g_sent, o_sent, d_sent, f_sent,
):
    blk, uly = lax.axis_index("blk"), lax.axis_index("uly")
    hi, x, z = blk // 16, (blk // 4) % 4, blk % 4
    me = hi * 4 + uly
    role = lax.rem(hi + uly // 2, 2)

    def column(member):
        return ((member // 4) * 16 + x * 4 + z, member % 4)

    def along_x(step):
        return (hi * 16 + lax.rem(x + step, 4) * 4 + z, uly)

    def along_z(step):
        return (hi * 16 + x * 4 + lax.rem(z + step, 4), uly)

    def remote(src, dst, sent, arrived, to):
        return pltpu.make_async_remote_copy(src, dst, sent, arrived, device_id=to, device_id_type=MESH)

    def wait_for(ref, sem):
        pltpu.make_async_copy(ref, ref, sem).wait()

    barrier = pltpu.get_barrier_semaphore()
    for step in range(1, 8):
        pl.semaphore_signal(barrier, inc=1, device_id=column(lax.rem(me + step, 8)), device_id_type=MESH)
    for step in (1, 2, 3):
        pl.semaphore_signal(barrier, inc=1, device_id=along_z(step), device_id_type=MESH)
    for step in (1, 3):
        pl.semaphore_signal(barrier, inc=1, device_id=along_x(step), device_id_type=MESH)

    def unit_lanes(unit, group=None):
        first, count = UNITS[unit][2:]
        if group is None:
            return pl.ds(first * HD, count * HD)
        return pl.ds(pl.multiple_of(group * WIDTH + first * HD, HD), count * HD)

    def y_start(unit):
        lanes = unit_lanes(unit)
        rows = pl.ds(pl.multiple_of(hi * SHARD, SHARD), SHARD)
        first, count = UNITS[unit][:2]
        cond = []
        if first == 0:
            cond.append((q_hbm.at[:, lanes], qkv.at[0, rows, lanes]))
        if first + count > 1:
            low = max(first, 1)
            span = first + count - low
            cond.append((kv_hbm.at[pl.ds(low - 1, span), :, lanes], qkv.at[pl.ds(low, span), rows, lanes]))
        arrays = pl.ds(first, count)
        piece = qkv.at[arrays, pl.ds(pl.multiple_of(me * PIECE, PIECE), PIECE), lanes]

        @pl.when(role == 0)
        def _():
            for src, dst in cond:
                pltpu.make_async_copy(src, dst, y_sem.at[unit]).start()

        @pl.when(role == 1)
        def _():
            for src, dst in cond:
                remote(src, dst, y_sent, y_sem.at[unit], column((uly // 2) * 4 + uly)).start()
            pltpu.make_async_copy(qkv_hbm.at[arrays, :, unit_lanes(unit, uly)], piece, y_sem.at[unit]).start()

        for group in range(4):
            owner = (1 - group // 2) * 4 + group

            @pl.when(me != owner)
            def _():
                remote(
                    qkv_hbm.at[arrays, :, unit_lanes(unit, group)], piece, y_sent, y_sem.at[unit],
                    column(owner)).start()

    def y_wait(unit):
        wait_for(qkv.at[pl.ds(*UNITS[unit][:2]), slot_rows(0), unit_lanes(unit)], y_sem.at[unit])

    def y_settle():
        @pl.when(role == 0)
        def _():
            wait_for(qkv.at[:, pl.ds(0, SHARD), :], y_sent)

        @pl.when(role == 1)
        def _():
            wait_for(qkv.at[:, pl.ds(0, PAIR - PIECE), :], y_sent)

    def gathered(kind, head, rows, arrays=None):
        return qkv.at[0 if kind == 0 else pl.ds(1, 2) if arrays is None else arrays, rows, head_lanes(head)]

    def gather(kind, head, order, arrays=None):
        for step, slot, row in ((1, 1, 0), (3, 3, SHARD)):
            if order == 0:
                src, dst = slot_rows(0), slot_rows(slot)
            else:
                src, dst = pl.ds(slot * PAIR + row, SHARD), pl.ds(2 * PAIR + row, SHARD)
            remote(
                gathered(kind, head, src, arrays), gathered(kind, head, dst, arrays), g_sent.at[kind],
                g_sem.at[head, kind, order], along_z(step) if kind == 0 else along_x(step)).start()

    def gather_wait(kind, head, order):
        wait_for(gathered(kind, head, pl.ds(0, (2 - order) * PAIR)), g_sem.at[head, kind, order])

    def direct(slot):
        to = along_z(STEPS[slot])
        into = STEPS[slot] - 1
        remote(o_send.at[LAST, :, slot_rows(slot)], o_recv.at[into], d_sent.at[0], d_sem.at[0], to).start()
        remote(st_send.at[LAST, slot], st_recv.at[into], d_sent.at[1], d_sem.at[1], to).start()

    def hand_over(head, stage_of):
        for side, step in ((0, 1), (1, 3)):
            if stage_of == 0:
                data = (o_send.at[head, pl.ds(side * HALF, HALF), slot_rows(2)], o_half_in.at[head, side])
                note = (st_send.at[head, 2], st_half_in.at[head, side])
            else:
                data = (o_full.at[head, side], o_full_in.at[head, side])
                note = (st_full.at[head, side], st_full_in.at[head, side])
            for i, (src, dst) in enumerate((data, note)):
                remote(src, dst, o_sent.at[stage_of, i], o_sem.at[head, stage_of, i], along_z(step)).start()

    def give_back(part):
        first, count = RETURNS[part]
        src_lanes = pl.ds(first * HD, count * HD)
        dst_lanes = pl.ds(pl.multiple_of(uly * WIDTH + first * HD, HD), count * HD)

        def refs(target):
            rows = pl.ds(pl.multiple_of(target * PIECE, PIECE), PIECE)
            return stage.at[rows, src_lanes], tokens.at[role, :, dst_lanes]

        for step in range(1, 8):
            target = lax.rem(me + step, 8)
            src, dst = refs(target)
            remote(src, dst, f_sent, f_sem.at[part], column(target)).start()
        src, dst = refs(me)
        pltpu.make_async_copy(src, dst, f_sem.at[part]).start()

    def prepare():
        lane = lax.broadcasted_iota(jnp.int32, (SHARD, HD), 1)
        row = lax.broadcasted_iota(jnp.int32, (SHARD, HD), 0)
        for slot in range(4):
            for half in range(2):
                present = valid_ref[half * 16 + lax.rem(x + 4 - slot, 4) * 4 + z]
                block = jnp.where((row >= present) & (lane == 0), UNUSABLE, 0.0)
                bias[pl.ds(slot * PAIR + half * SHARD, SHARD), :] = block.astype(jnp.bfloat16)
        ones[...] = jnp.where(
            lax.broadcasted_iota(jnp.int32, (TILE, HD), 1) == 0, 1.0, 0.0).astype(jnp.bfloat16)
        vt[pl.ds(HD, 16), :] = jnp.ones((16, ALL), jnp.bfloat16)

    def transpose_values(head, slots):
        rows = lax.broadcasted_iota(jnp.int32, (HD, HD), 0)
        lanes = lax.broadcasted_iota(jnp.int32, (HD, HD), 1)
        eye = (rows == lanes).astype(jnp.bfloat16)
        for slot in slots:
            vt[pl.ds(0, HD), slot_rows(slot)] = lax.dot_general(
                eye, qkv[2, slot_rows(slot), head_lanes(head)], NT,
                preferred_element_type=jnp.float32).astype(jnp.bfloat16)

    def attend_slots(head, slots, combine, store):
        buffers = (scores_even, scores_odd)
        starts = [i * TILE for i in (3, 4, 5, 2, 1, 0)]

        def scored(i, k):
            queries = jnp.concatenate([qkv[0, pl.ds(starts[i], TILE), head_lanes(head)], ones[...]], axis=1)
            keys = jnp.concatenate([qkv[1, slot_rows(slots[k]), head_lanes(head)], bias[slot_rows(slots[k]), :]], axis=1)
            part = lax.dot_general(keys, queries, NT, preferred_element_type=jnp.float32)
            buffers[i % 2][slot_rows(k), :] = part
            return jnp.max(part.reshape(PAIR // 8, 8, TILE), axis=0)

        def weighted(i, k, top):
            weights = jnp.exp2((buffers[i % 2][slot_rows(k), :] - top) * SCALE).astype(jnp.bfloat16)
            return jnp.dot(vt[:, slot_rows(slots[k])], weights, preferred_element_type=jnp.float32)

        def whole(parts):
            return jnp.max(functools.reduce(jnp.maximum, parts), axis=0, keepdims=True)

        top = whole([scored(0, k) for k in range(len(slots))])
        for i, start in enumerate(starts):
            lanes = pl.ds(start, TILE)
            top = combine(lanes, top)
            total, next_tops = None, []
            for k in range(len(slots)):
                if i + 1 < len(starts):
                    next_tops.append(scored(i + 1, k))
                part = weighted(i, k, top)
                total = part if total is None else total + part
            store(i, lanes, top, total)
            if next_tops:
                top = whole(next_tops)

    def packed(top, total):
        rows = [row[:, i * HD:(i + 1) * HD] for row in (top, total) for i in range(3)]
        return jnp.concatenate(rows + [jnp.zeros((2, HD), jnp.float32)], axis=0)

    def unpacked(block):
        return tuple(
            jnp.concatenate([block[k + i:k + i + 1] for i in range(3)], axis=1) for k in (0, 3))

    def near_keys(head):
        transpose_values(head, (0, 1, 3))

        def store(i, lanes, top, total):
            partial[:, lanes] = total
            tops[:, lanes] = top

        attend_slots(head, (0, 1, 3), lambda lanes, top: top, store)

    def far_keys(head):
        transpose_values(head, (2,))

        def combine(lanes, top):
            return jnp.maximum(top, tops[:, lanes])

        def store(i, lanes, top, total):
            total = total + partial[:, lanes] * jnp.exp2((tops[:, lanes] - top) * SCALE)
            o_send[head, :, lanes] = total[:HD].astype(jnp.bfloat16)
            stats[pl.ds(0, 1), lanes] = top
            stats[pl.ds(1, 1), lanes] = total[HD:HD + 1]
            slot = {1: 2, 2: 3, 4: 1, 5: 0}.get(i)
            if slot is not None:
                st_send[head, slot] = packed(
                    stats[pl.ds(0, 1), slot_rows(slot)], stats[pl.ds(1, 1), slot_rows(slot)])
            if slot == 2:
                @pl.when(head < LAST)
                def _():
                    hand_over(head, 0)
            if slot:
                @pl.when(head == LAST)
                def _():
                    direct(slot)

        attend_slots(head, (2,), combine, store)

    def pass_on(head):
        wait_for(o_half_in.at[head], o_sem.at[head, 0, 0])
        wait_for(st_half_in.at[head], o_sem.at[head, 0, 1])
        for side, slot in ((0, 3), (1, 1)):
            own_top, own_sum = unpacked(st_send[head, slot])
            in_top, in_sum = unpacked(st_half_in[head, side])
            top = jnp.maximum(own_top, in_top)
            own_factor, in_factor = jnp.exp2((own_top - top) * SCALE), jnp.exp2((in_top - top) * SCALE)
            for half in range(2):
                rows = pl.ds(half * HALF, HALF)
                block = o_send[head, rows, slot_rows(slot)].astype(jnp.float32) * own_factor
                if half == side:
                    block = block + o_half_in[head, side].astype(jnp.float32) * in_factor
                o_full[head, side, rows] = block.astype(jnp.bfloat16)
            total = own_sum * own_factor
            if side == 0:
                total = total + in_sum * in_factor
            st_full[head, side] = packed(top, total)
        hand_over(head, 1)

    def merge(head):
        if isinstance(head, int) and head == LAST:
            wait_for(o_recv, d_sem.at[0])
            wait_for(st_recv, d_sem.at[1])
            arrived = [(o_recv[i], st_recv[i]) for i in range(3)]
        else:
            wait_for(o_full_in.at[head], o_sem.at[head, 1, 0])
            wait_for(st_full_in.at[head], o_sem.at[head, 1, 1])
            arrived = [(o_full_in[head, side], st_full_in[head, side]) for side in range(2)]
        arrived.append((o_send[head, :, slot_rows(0)], st_send[head, 0]))
        pairs = [unpacked(block) for _, block in arrived]
        top = functools.reduce(jnp.maximum, [pair[0] for pair in pairs])
        factors = [jnp.exp2((pair[0] - top) * SCALE) for pair in pairs]
        denominator = sum(f * pair[1] for f, pair in zip(factors, pairs))
        numerator = sum(f * block.astype(jnp.float32) for f, (block, _) in zip(factors, arrived))
        stage[:, head_lanes(head)] = (numerator / denominator).T.astype(jnp.bfloat16)

    def spread(head):
        for kind in range(2):
            gather(kind, head, 0)

    def relay(head):
        for kind in range(2):
            gather_wait(kind, head, 0)
            gather(kind, head, 1)

    def head_step(head, _):
        gather_wait(0, head, 1)
        near_keys(head)

        @pl.when(head < LAST)
        def _():
            relay(head + 1)

        @pl.when(head >= 1)
        def _():
            pass_on(head - 1)

        gather_wait(1, head, 1)
        far_keys(head)

        @pl.when(head == 0)
        def _():
            y_wait(5)

        @pl.when(head + 3 < HEADS)
        def _():
            spread(head + 3)

        @pl.when(head >= 2)
        def _():
            merge(head - 2)

        @pl.when(head == 3)
        def _():
            give_back(0)

        @pl.when(head == 4)
        def _():
            give_back(1)

        return 0

    pl.semaphore_wait(barrier, 12)
    for unit in range(len(UNITS)):
        y_start(unit)
    prepare()
    y_wait(0)
    gather(1, 0, 0, 1)
    y_wait(1)
    gather(1, 0, 0, 2)
    y_wait(2)
    gather(0, 0, 0)
    y_wait(3)
    spread(1)
    relay(0)
    y_wait(4)
    spread(2)
    lax.fori_loop(0, HEADS, head_step, 0)
    merge(LAST - 1)
    give_back(2)
    y_settle()
    wait_for(qkv.at[0, pl.ds(0, 3 * PAIR), :], g_sent.at[0])
    wait_for(qkv.at[pl.ds(1, 2), pl.ds(0, 3 * PAIR), :], g_sent.at[1])
    for i, (data, note) in enumerate(((o_half_in, st_half_in), (o_full, st_full))):
        wait_for(data, o_sent.at[i, 0])
        wait_for(note, o_sent.at[i, 1])
    merge(LAST)
    give_back(3)
    lanes = lax.broadcasted_iota(jnp.int32, (PIECE, PIECE), 1)
    rows = lax.broadcasted_iota(jnp.int32, (PIECE, PIECE), 0)
    chosen = jnp.where((rows == lanes) & (refresh_ref[...] == 1), 1.0, 0.0).astype(jnp.bfloat16)
    renew = jnp.dot(chosen, jnp.ones((PIECE, HD), jnp.bfloat16), preferred_element_type=jnp.float32) > 0.5
    for part, (first, count) in enumerate(RETURNS):
        if part == len(RETURNS) - 1:
            wait_for(o_recv, d_sent.at[0])
            wait_for(st_recv, d_sent.at[1])
            wait_for(stage.at[pl.ds(0, PAIR - PIECE), :], f_sent)
        wait_for(tokens.at[:, :, pl.ds(0, 4 * count * HD)], f_sem.at[part])
        for block in (group * HEADS + first + i for group in range(4) for i in range(count)):
            columns = pl.ds(block * HD, HD)
            kept = cache_ref[:, columns].astype(jnp.float32)
            kept = jnp.where(renew, tokens[1, :, columns].astype(jnp.float32), kept)
            cache_out[:, columns] = kept.astype(jnp.bfloat16)
            guided = kept + GUIDANCE * (tokens[0, :, columns].astype(jnp.float32) - kept)
            guided_out[:, columns] = guided.astype(jnp.bfloat16)


def on_device(cond_query, cond_kv, uncond_qkv, uncond_cache, refresh, valid):
    any_space = pl.BlockSpec(memory_space=pl.ANY)
    vmem = pl.BlockSpec(memory_space=pltpu.VMEM)
    dma = pltpu.SemaphoreType.DMA
    bf16, f32 = jnp.bfloat16, jnp.float32
    result = jax.ShapeDtypeStruct((PIECE, 4 * WIDTH), bf16)
    return pl.pallas_call(
        kernel,
        out_shape=(result, result),
        in_specs=[pl.BlockSpec(memory_space=pltpu.SMEM), any_space, any_space, any_space, vmem, vmem],
        out_specs=(vmem, vmem),
        scratch_shapes=[
            pltpu.VMEM((3, ALL, WIDTH), bf16),
            pltpu.VMEM((HD + 16, ALL), bf16),
            pltpu.VMEM((ALL, HD), bf16),
            pltpu.VMEM((TILE, HD), bf16),
            pltpu.VMEM((3 * PAIR, TILE), f32),
            pltpu.VMEM((3 * PAIR, TILE), f32),
            pltpu.VMEM((HD + 16, ALL), f32),
            pltpu.VMEM((1, ALL), f32),
            pltpu.VMEM((8, ALL), f32),
            pltpu.VMEM((HEADS, HD, ALL), bf16),
            pltpu.VMEM((HEADS, 4, 8, HD), f32),
            pltpu.VMEM((LAST, 2, HALF, PAIR), bf16),
            pltpu.VMEM((LAST, 2, 8, HD), f32),
            pltpu.VMEM((LAST, 2, HD, PAIR), bf16),
            pltpu.VMEM((LAST, 2, HD, PAIR), bf16),
            pltpu.VMEM((LAST, 2, 8, HD), f32),
            pltpu.VMEM((LAST, 2, 8, HD), f32),
            pltpu.VMEM((3, HD, PAIR), bf16),
            pltpu.VMEM((3, 8, HD), f32),
            pltpu.VMEM((PAIR, WIDTH), bf16),
            pltpu.VMEM((2, PIECE, 4 * WIDTH), bf16),
            dma((len(UNITS),)), dma((HEADS, 2, 2)), dma((LAST, 2, 2)), dma((2,)), dma((len(RETURNS),)),
            dma, dma((2,)), dma((2, 2)), dma((2,)), dma,
        ],
        compiler_params=pltpu.CompilerParams(
            collective_id=0, has_side_effects=True, vmem_limit_bytes=54592 << 10)
    )(valid, cond_query, cond_kv, uncond_qkv, uncond_cache, refresh.reshape(1, PIECE))


def solution(mesh):
    placed = (
        P("blk", "uly"),
        P(None, "blk", "uly"),
        P(None, ("blk", "uly"), None),
        P(("blk", "uly"), None),
        P(("blk", "uly")),
        P(),
    )
    return jax.shard_map(
        on_device,
        mesh=mesh,
        in_specs=placed,
        out_specs=(P(("blk", "uly"), None), P(("blk", "uly"), None)),
        check_vma=False,
    )
```

```python
import functools

import jax
import jax.numpy as jnp
from jax import lax
from jax.experimental import pallas as pl
from jax.experimental.pallas import tpu as pltpu
from jax.sharding import PartitionSpec as P

HD = 128
GUIDANCE = 5.0
MESH = pl.DeviceIdType.MESH
LOG2E = 1.4426950408889634
SCALE = LOG2E * HD ** (-0.5)
UNUSABLE = -1e30

HALF = HD // 2
HEADS = 5
LAST = HEADS - 1
WIDTH = HEADS * HD
UNITS = ((1, 1, 0, 1), (2, 1, 0, 1), (0, 1, 0, 1), (0, 3, 1, 1), (0, 3, 2, 1), (0, 3, 3, 1), (0, 3, 4, 1))
RETURNS = ((0, 2), (2, 1), (3, 1), (4, 1))
SHARD = 192
PIECE = 48
PAIR = 2 * SHARD
ALL = 4 * PAIR
TILE = 256
NT = (((1,), (1,)), ((), ()))
STEPS = (0, 3, 2, 1)


def slot_rows(slot):
    return pl.ds(slot * PAIR, PAIR)


def head_lanes(head):
    return pl.ds(pl.multiple_of(head * HD, HD), HD)


def kernel(
    valid_ref, q_hbm, kv_hbm, qkv_hbm, cache_ref, refresh_ref, guided_out, cache_out,
    qkv, vt, bias, ones, scores_even, scores_odd, partial, tops, stats,
    o_send, st_send, o_half_in, st_half_in, o_full, o_full_in, st_full, st_full_in, o_recv, st_recv, stage, tokens,
    y_sem, g_sem, o_sem, d_sem, f_sem, y_sent, g_sent, o_sent, d_sent, f_sent,
):
    blk, uly = lax.axis_index("blk"), lax.axis_index("uly")
    hi, x, z = blk // 16, (blk // 4) % 4, blk % 4
    me = hi * 4 + uly
    role = lax.rem(hi + uly // 2, 2)

    def column(member):
        return ((member // 4) * 16 + x * 4 + z, member % 4)

    def along_x(step):
        return (hi * 16 + lax.rem(x + step, 4) * 4 + z, uly)

    def along_z(step):
        return (hi * 16 + x * 4 + lax.rem(z + step, 4), uly)

    def remote(src, dst, sent, arrived, to):
        return pltpu.make_async_remote_copy(src, dst, sent, arrived, device_id=to, device_id_type=MESH)

    def wait_for(ref, sem):
        pltpu.make_async_copy(ref, ref, sem).wait()

    barrier = pltpu.get_barrier_semaphore()
    for step in range(1, 8):
        pl.semaphore_signal(barrier, inc=1, device_id=column(lax.rem(me + step, 8)), device_id_type=MESH)
    for step in (1, 2, 3):
        pl.semaphore_signal(barrier, inc=1, device_id=along_z(step), device_id_type=MESH)
    for step in (1, 3):
        pl.semaphore_signal(barrier, inc=1, device_id=along_x(step), device_id_type=MESH)

    def unit_lanes(unit, group=None):
        first, count = UNITS[unit][2:]
        if group is None:
            return pl.ds(first * HD, count * HD)
        return pl.ds(pl.multiple_of(group * WIDTH + first * HD, HD), count * HD)

    def y_start(unit):
        lanes = unit_lanes(unit)
        rows = pl.ds(pl.multiple_of(hi * SHARD, SHARD), SHARD)
        first, count = UNITS[unit][:2]
        cond = []
        if first == 0:
            cond.append((q_hbm.at[:, lanes], qkv.at[0, rows, lanes]))
        if first + count > 1:
            low = max(first, 1)
            span = first + count - low
            cond.append((kv_hbm.at[pl.ds(low - 1, span), :, lanes], qkv.at[pl.ds(low, span), rows, lanes]))
        arrays = pl.ds(first, count)
        piece = qkv.at[arrays, pl.ds(pl.multiple_of(me * PIECE, PIECE), PIECE), lanes]

        @pl.when(role == 0)
        def _():
            for src, dst in cond:
                pltpu.make_async_copy(src, dst, y_sem.at[unit]).start()

        @pl.when(role == 1)
        def _():
            for src, dst in cond:
                remote(src, dst, y_sent, y_sem.at[unit], column((uly // 2) * 4 + uly)).start()
            pltpu.make_async_copy(qkv_hbm.at[arrays, :, unit_lanes(unit, uly)], piece, y_sem.at[unit]).start()

        for group in range(4):
            owner = (1 - group // 2) * 4 + group

            @pl.when(me != owner)
            def _():
                remote(
                    qkv_hbm.at[arrays, :, unit_lanes(unit, group)], piece, y_sent, y_sem.at[unit],
                    column(owner)).start()

    def y_wait(unit):
        wait_for(qkv.at[pl.ds(*UNITS[unit][:2]), slot_rows(0), unit_lanes(unit)], y_sem.at[unit])

    def y_settle():
        @pl.when(role == 0)
        def _():
            wait_for(qkv.at[:, pl.ds(0, SHARD), :], y_sent)

        @pl.when(role == 1)
        def _():
            wait_for(qkv.at[:, pl.ds(0, PAIR - PIECE), :], y_sent)

    def gathered(kind, head, rows, arrays=None):
        return qkv.at[0 if kind == 0 else pl.ds(1, 2) if arrays is None else arrays, rows, head_lanes(head)]

    def gather(kind, head, order, arrays=None):
        for step, slot, row in ((1, 1, 0), (3, 3, SHARD)):
            if order == 0:
                src, dst = slot_rows(0), slot_rows(slot)
            else:
                src, dst = pl.ds(slot * PAIR + row, SHARD), pl.ds(2 * PAIR + row, SHARD)
            remote(
                gathered(kind, head, src, arrays), gathered(kind, head, dst, arrays), g_sent.at[kind],
                g_sem.at[head, kind, order], along_z(step) if kind == 0 else along_x(step)).start()

    def gather_wait(kind, head, order):
        wait_for(gathered(kind, head, pl.ds(0, (2 - order) * PAIR)), g_sem.at[head, kind, order])

    def direct(slot):
        to = along_z(STEPS[slot])
        into = STEPS[slot] - 1
        remote(o_send.at[LAST, :, slot_rows(slot)], o_recv.at[into], d_sent.at[0], d_sem.at[0], to).start()
        remote(st_send.at[LAST, slot], st_recv.at[into], d_sent.at[1], d_sem.at[1], to).start()

    def hand_over(head, stage_of):
        for side, step in ((0, 1), (1, 3)):
            if stage_of == 0:
                data = (o_send.at[head, pl.ds(side * HALF, HALF), slot_rows(2)], o_half_in.at[head, side])
                note = (st_send.at[head, 2], st_half_in.at[head, side])
            else:
                data = (o_full.at[head, side], o_full_in.at[head, side])
                note = (st_full.at[head, side], st_full_in.at[head, side])
            for i, (src, dst) in enumerate((data, note)):
                remote(src, dst, o_sent.at[stage_of, i], o_sem.at[head, stage_of, i], along_z(step)).start()

    def give_back(part):
        first, count = RETURNS[part]
        src_lanes = pl.ds(first * HD, count * HD)
        dst_lanes = pl.ds(pl.multiple_of(uly * WIDTH + first * HD, HD), count * HD)

        def refs(target):
            rows = pl.ds(pl.multiple_of(target * PIECE, PIECE), PIECE)
            return stage.at[rows, src_lanes], tokens.at[role, :, dst_lanes]

        for step in range(1, 8):
            target = lax.rem(me + step, 8)
            src, dst = refs(target)
            remote(src, dst, f_sent, f_sem.at[part], column(target)).start()
        src, dst = refs(me)
        pltpu.make_async_copy(src, dst, f_sem.at[part]).start()

    def prepare():
        lane = lax.broadcasted_iota(jnp.int32, (SHARD, HD), 1)
        row = lax.broadcasted_iota(jnp.int32, (SHARD, HD), 0)
        for slot in range(4):
            for half in range(2):
                present = valid_ref[half * 16 + lax.rem(x + 4 - slot, 4) * 4 + z]
                block = jnp.where((row >= present) & (lane == 0), UNUSABLE, 0.0)
                bias[pl.ds(slot * PAIR + half * SHARD, SHARD), :] = block.astype(jnp.bfloat16)
        ones[...] = jnp.where(
            lax.broadcasted_iota(jnp.int32, (TILE, HD), 1) == 0, 1.0, 0.0).astype(jnp.bfloat16)
        vt[pl.ds(HD, 16), :] = jnp.ones((16, ALL), jnp.bfloat16)

    def transpose_values(head, slots):
        rows = lax.broadcasted_iota(jnp.int32, (HD, HD), 0)
        lanes = lax.broadcasted_iota(jnp.int32, (HD, HD), 1)
        eye = (rows == lanes).astype(jnp.bfloat16)
        for slot in slots:
            vt[pl.ds(0, HD), slot_rows(slot)] = lax.dot_general(
                eye, qkv[2, slot_rows(slot), head_lanes(head)], NT,
                preferred_element_type=jnp.float32).astype(jnp.bfloat16)

    def attend_slots(head, slots, combine, store):
        buffers = (scores_even, scores_odd)
        starts = [i * TILE for i in (3, 4, 5, 2, 1, 0)]

        def scored(i, k):
            queries = jnp.concatenate([qkv[0, pl.ds(starts[i], TILE), head_lanes(head)], ones[...]], axis=1)
            keys = jnp.concatenate([qkv[1, slot_rows(slots[k]), head_lanes(head)], bias[slot_rows(slots[k]), :]], axis=1)
            part = lax.dot_general(keys, queries, NT, preferred_element_type=jnp.float32)
            buffers[i % 2][slot_rows(k), :] = part
            return jnp.max(part.reshape(PAIR // 8, 8, TILE), axis=0)

        def weighted(i, k, top):
            weights = jnp.exp2((buffers[i % 2][slot_rows(k), :] - top) * SCALE).astype(jnp.bfloat16)
            return jnp.dot(vt[:, slot_rows(slots[k])], weights, preferred_element_type=jnp.float32)

        def whole(parts):
            return jnp.max(functools.reduce(jnp.maximum, parts), axis=0, keepdims=True)

        top = whole([scored(0, k) for k in range(len(slots))])
        for i, start in enumerate(starts):
            lanes = pl.ds(start, TILE)
            top = combine(lanes, top)
            total, next_tops = None, []
            for k in range(len(slots)):
                if i + 1 < len(starts):
                    next_tops.append(scored(i + 1, k))
                part = weighted(i, k, top)
                total = part if total is None else total + part
            store(i, lanes, top, total)
            if next_tops:
                top = whole(next_tops)

    def packed(top, total):
        rows = [row[:, i * HD:(i + 1) * HD] for row in (top, total) for i in range(3)]
        return jnp.concatenate(rows + [jnp.zeros((2, HD), jnp.float32)], axis=0)

    def unpacked(block):
        return tuple(
            jnp.concatenate([block[k + i:k + i + 1] for i in range(3)], axis=1) for k in (0, 3))

    def near_keys(head):
        transpose_values(head, (0, 1, 3))

        def store(i, lanes, top, total):
            partial[:, lanes] = total
            tops[:, lanes] = top

        attend_slots(head, (0, 1, 3), lambda lanes, top: top, store)

    def far_keys(head):
        transpose_values(head, (2,))

        def combine(lanes, top):
            return jnp.maximum(top, tops[:, lanes])

        def store(i, lanes, top, total):
            total = total + partial[:, lanes] * jnp.exp2((tops[:, lanes] - top) * SCALE)
            o_send[head, :, lanes] = total[:HD].astype(jnp.bfloat16)
            stats[pl.ds(0, 1), lanes] = top
            stats[pl.ds(1, 1), lanes] = total[HD:HD + 1]
            slot = {1: 2, 2: 3, 4: 1, 5: 0}.get(i)
            if slot is not None:
                st_send[head, slot] = packed(
                    stats[pl.ds(0, 1), slot_rows(slot)], stats[pl.ds(1, 1), slot_rows(slot)])
            if slot == 2:
                @pl.when(head < LAST)
                def _():
                    hand_over(head, 0)
            if slot:
                @pl.when(head == LAST)
                def _():
                    direct(slot)

        attend_slots(head, (2,), combine, store)

    def pass_on(head):
        wait_for(o_half_in.at[head], o_sem.at[head, 0, 0])
        wait_for(st_half_in.at[head], o_sem.at[head, 0, 1])
        for side, slot in ((0, 3), (1, 1)):
            own_top, own_sum = unpacked(st_send[head, slot])
            in_top, in_sum = unpacked(st_half_in[head, side])
            top = jnp.maximum(own_top, in_top)
            own_factor, in_factor = jnp.exp2((own_top - top) * SCALE), jnp.exp2((in_top - top) * SCALE)
            for half in range(2):
                rows = pl.ds(half * HALF, HALF)
                block = o_send[head, rows, slot_rows(slot)].astype(jnp.float32) * own_factor
                if half == side:
                    block = block + o_half_in[head, side].astype(jnp.float32) * in_factor
                o_full[head, side, rows] = block.astype(jnp.bfloat16)
            total = own_sum * own_factor
            if side == 0:
                total = total + in_sum * in_factor
            st_full[head, side] = packed(top, total)
        hand_over(head, 1)

    def merge(head):
        if isinstance(head, int) and head == LAST:
            wait_for(o_recv, d_sem.at[0])
            wait_for(st_recv, d_sem.at[1])
            arrived = [(o_recv[i], st_recv[i]) for i in range(3)]
        else:
            wait_for(o_full_in.at[head], o_sem.at[head, 1, 0])
            wait_for(st_full_in.at[head], o_sem.at[head, 1, 1])
            arrived = [(o_full_in[head, side], st_full_in[head, side]) for side in range(2)]
        arrived.append((o_send[head, :, slot_rows(0)], st_send[head, 0]))
        pairs = [unpacked(block) for _, block in arrived]
        top = functools.reduce(jnp.maximum, [pair[0] for pair in pairs])
        factors = [jnp.exp2((pair[0] - top) * SCALE) for pair in pairs]
        denominator = sum(f * pair[1] for f, pair in zip(factors, pairs))
        numerator = sum(f * block.astype(jnp.float32) for f, (block, _) in zip(factors, arrived))
        stage[:, head_lanes(head)] = (numerator / denominator).T.astype(jnp.bfloat16)

    def spread(head):
        for kind in range(2):
            gather(kind, head, 0)

    def relay(head):
        for kind in range(2):
            gather_wait(kind, head, 0)
            gather(kind, head, 1)

    def head_step(head, _):
        gather_wait(0, head, 1)
        near_keys(head)

        @pl.when(head < LAST)
        def _():
            relay(head + 1)

        @pl.when(head >= 1)
        def _():
            pass_on(head - 1)

        gather_wait(1, head, 1)
        far_keys(head)

        @pl.when(head + 3 < HEADS)
        def _():
            wait_for(qkv.at[:, slot_rows(0), head_lanes(head + 3)], y_sem.at[head + 5])
            spread(head + 3)

        @pl.when(head >= 2)
        def _():
            merge(head - 2)

        @pl.when(head == 3)
        def _():
            give_back(0)

        @pl.when(head == 4)
        def _():
            give_back(1)

        return 0

    pl.semaphore_wait(barrier, 12)
    for unit in range(len(UNITS)):
        y_start(unit)
    prepare()
    y_wait(0)
    gather(1, 0, 0, 1)
    y_wait(1)
    gather(1, 0, 0, 2)
    y_wait(2)
    gather(0, 0, 0)
    y_wait(3)
    spread(1)
    relay(0)
    y_wait(4)
    spread(2)
    lax.fori_loop(0, HEADS, head_step, 0)
    merge(LAST - 1)
    give_back(2)
    y_settle()
    wait_for(qkv.at[0, pl.ds(0, 3 * PAIR), :], g_sent.at[0])
    wait_for(qkv.at[pl.ds(1, 2), pl.ds(0, 3 * PAIR), :], g_sent.at[1])
    for i, (data, note) in enumerate(((o_half_in, st_half_in), (o_full, st_full))):
        wait_for(data, o_sent.at[i, 0])
        wait_for(note, o_sent.at[i, 1])
    merge(LAST)
    give_back(3)
    lanes = lax.broadcasted_iota(jnp.int32, (PIECE, PIECE), 1)
    rows = lax.broadcasted_iota(jnp.int32, (PIECE, PIECE), 0)
    chosen = jnp.where((rows == lanes) & (refresh_ref[...] == 1), 1.0, 0.0).astype(jnp.bfloat16)
    renew = jnp.dot(chosen, jnp.ones((PIECE, HD), jnp.bfloat16), preferred_element_type=jnp.float32) > 0.5
    for part, (first, count) in enumerate(RETURNS):
        if part == len(RETURNS) - 1:
            wait_for(o_recv, d_sent.at[0])
            wait_for(st_recv, d_sent.at[1])
            wait_for(stage.at[pl.ds(0, PAIR - PIECE), :], f_sent)
        wait_for(tokens.at[:, :, pl.ds(0, 4 * count * HD)], f_sem.at[part])
        for block in (group * HEADS + first + i for group in range(4) for i in range(count)):
            columns = pl.ds(block * HD, HD)
            kept = cache_ref[:, columns].astype(jnp.float32)
            kept = jnp.where(renew, tokens[1, :, columns].astype(jnp.float32), kept)
            cache_out[:, columns] = kept.astype(jnp.bfloat16)
            guided = kept + GUIDANCE * (tokens[0, :, columns].astype(jnp.float32) - kept)
            guided_out[:, columns] = guided.astype(jnp.bfloat16)


def on_device(cond_query, cond_kv, uncond_qkv, uncond_cache, refresh, valid):
    any_space = pl.BlockSpec(memory_space=pl.ANY)
    vmem = pl.BlockSpec(memory_space=pltpu.VMEM)
    dma = pltpu.SemaphoreType.DMA
    bf16, f32 = jnp.bfloat16, jnp.float32
    result = jax.ShapeDtypeStruct((PIECE, 4 * WIDTH), bf16)
    return pl.pallas_call(
        kernel,
        out_shape=(result, result),
        in_specs=[pl.BlockSpec(memory_space=pltpu.SMEM), any_space, any_space, any_space, vmem, vmem],
        out_specs=(vmem, vmem),
        scratch_shapes=[
            pltpu.VMEM((3, ALL, WIDTH), bf16),
            pltpu.VMEM((HD + 16, ALL), bf16),
            pltpu.VMEM((ALL, HD), bf16),
            pltpu.VMEM((TILE, HD), bf16),
            pltpu.VMEM((3 * PAIR, TILE), f32),
            pltpu.VMEM((3 * PAIR, TILE), f32),
            pltpu.VMEM((HD + 16, ALL), f32),
            pltpu.VMEM((1, ALL), f32),
            pltpu.VMEM((8, ALL), f32),
            pltpu.VMEM((HEADS, HD, ALL), bf16),
            pltpu.VMEM((HEADS, 4, 8, HD), f32),
            pltpu.VMEM((LAST, 2, HALF, PAIR), bf16),
            pltpu.VMEM((LAST, 2, 8, HD), f32),
            pltpu.VMEM((LAST, 2, HD, PAIR), bf16),
            pltpu.VMEM((LAST, 2, HD, PAIR), bf16),
            pltpu.VMEM((LAST, 2, 8, HD), f32),
            pltpu.VMEM((LAST, 2, 8, HD), f32),
            pltpu.VMEM((3, HD, PAIR), bf16),
            pltpu.VMEM((3, 8, HD), f32),
            pltpu.VMEM((PAIR, WIDTH), bf16),
            pltpu.VMEM((2, PIECE, 4 * WIDTH), bf16),
            dma((len(UNITS),)), dma((HEADS, 2, 2)), dma((LAST, 2, 2)), dma((2,)), dma((len(RETURNS),)),
            dma, dma((2,)), dma((2, 2)), dma((2,)), dma,
        ],
        compiler_params=pltpu.CompilerParams(
            collective_id=0, has_side_effects=True, vmem_limit_bytes=54592 << 10)
    )(valid, cond_query, cond_kv, uncond_qkv, uncond_cache, refresh.reshape(1, PIECE))


def solution(mesh):
    placed = (
        P("blk", "uly"),
        P(None, "blk", "uly"),
        P(None, ("blk", "uly"), None),
        P(("blk", "uly"), None),
        P(("blk", "uly")),
        P(),
    )
    return jax.shard_map(
        on_device,
        mesh=mesh,
        in_specs=placed,
        out_specs=(P(("blk", "uly"), None), P(("blk", "uly"), None)),
        check_vma=False,
    )
```
